128 devices in a mesh: row: 8 (over y, core), col: 16 (over x, z).
Axes of the slice: x: 4, y: 4, z: 4, core: 2. Of those that a mesh axis runs over, the one named last changes fastest.
Arguments:
- temp_thermal: float32 [16, 524288], P(None, ('row', 'col')), may hold values from -6 to 6
- send_index: int32 [128, 4096], P(('row', 'col')), may hold values from 0 to 4095
- interp_slot: int32 [4, 557056], P(None, ('row', 'col')), may hold values from 0 to 4095
- interp_weight: float32 [4, 557056], P(None, ('row', 'col')), may hold values from 0.1 to 1
- disp: bfloat16 [3, 16, 557056], P(None, None, ('row', 'col')), may hold values from -6 to 6
- expansion: float32 [3, 557056], P(None, ('row', 'col')), may hold values from -6 to 6
- tangent: bfloat16 [96, 96, 16384], P(None, None, ('row', 'col')), may hold values from -0.625 to 0.625
- connect: int32 [32, 16384], P(None, ('row', 'col')), may hold values from 0 to 4351
- recv_lower: int32 [16384], P(('row', 'col')), may hold values from 0 to 4095
- recv_upper: int32 [16384], P(('row', 'col')), may hold values from 0 to 4095
Outputs:
- residual: float32 [3, 16, 524288], P(None, None, ('row', 'col'))
The draws below stay inside these ranges and needn't reach their ends.
Inputs may be any that keep to these rules, and one draw needn't show every extreme that they name: `send_index`: local thermal node indices of the sending partition. `interp_slot`: slots of the subdomain's received thermal values. `connect`: subdomain-local node copies; below 4096 owned, then 128 lower ghosts, then 128 upper ghosts. `recv_lower`: owned nodes of the receiving subdomain. `recv_upper`: owned nodes of the receiving subdomain.
All inputs are finite; a program needn't handle non-finite values.
Results may differ from the reference program's by a relative error of at most 0.0029.
Values sent between devices are 32-bit elements; how exact they have to be, the bound alone decides.
No kernel may reach another device: no remote copies, remote signals or barrier semaphores. Data moves between devices by JAX's collectives and lax.ppermute only.
A program may use at most 64 MiB of HBM per device.

```python
import math
import jax
import jax.numpy as jnp
from jax import lax

SCEN = 16
NCL = 32
CLU_DEV = 128
RECV_DEV = 4096
NODE_DEV = 4096
GHOST = 128
EXT = 4352
TN_DEV = 4096
CLUSTERS = 16384
EXTS = 557056
TNODES = 524288
N_ROW = 8
N_COL = 16


def set_ends(entries, stream_key, low, largest):
    longest = entries.shape.index(max(entries.shape))
    spots = []
    for shift in (0, 1):
        where = [jax.random.randint(jax.random.fold_in(stream_key, axis), (), 0, length) for axis, length in enumerate(entries.shape)]
        where[longest] = (where[longest] + shift) % entries.shape[longest]
        spots.append(tuple(where))
    return entries.at[spots[0]].set(low).at[spots[1]].set(largest)


def shard_levels(key, shape, cuts, smallest, top_value):
    loudness, own = 1.0, jax.random.fold_in(key, 6)
    for dim, blocks in cuts:
        heights = jnp.exp(jax.random.uniform(jax.random.fold_in(own, dim), (blocks,), jnp.float32, smallest / len(cuts), top_value / len(cuts)))
        loudness = loudness * jnp.repeat(heights, shape[dim] // blocks).reshape([-1 if axis == dim else 1 for axis in range(len(shape))])
    return loudness


def centred(stream_key, shape, spread, limit, pieces=(), kind=jnp.bfloat16):
    array = spread * jax.random.normal(stream_key, shape, jnp.float32)
    if pieces:
        array = array * shard_levels(stream_key, shape, pieces, -0.22, 0.18)
    return jnp.clip(array, -limit, limit).astype(kind)


def setup_inputs(seed: int = 0) -> dict:
    seeds = jax.random.split(jax.random.key(seed), 11)
    return {
        "temp_thermal": centred(seeds[0], (SCEN, TNODES), 1.0, 6.0, ((1, 128),), jnp.float32),
        "send_index": set_ends(jax.random.randint(seeds[1], (N_ROW * N_COL, RECV_DEV), 0, TN_DEV), jax.random.fold_in(seeds[1], 1), 0, TN_DEV - 1).astype(jnp.int32),
        "interp_slot": set_ends(jax.random.randint(seeds[2], (4, EXTS), 0, RECV_DEV), jax.random.fold_in(seeds[2], 1), 0, RECV_DEV - 1).astype(jnp.int32),
        "interp_weight": jnp.clip(jnp.exp(math.log(1.0) - 2.3025851 * jax.random.uniform(seeds[3], (4, EXTS), jnp.float32) ** shard_levels(seeds[3], (4, EXTS), ((1, 128),), -0.2, 0.2)), 0.1, 1.0),
        "disp": centred(seeds[4], (3, SCEN, EXTS), 1.0, 6.0, ((2, 128),)),
        "expansion": centred(seeds[5], (3, EXTS), 1.0, 6.0, ((1, 128),), jnp.float32),
        "tangent": centred(seeds[6], (3 * NCL, 3 * NCL, CLUSTERS), (3 * NCL) ** -0.5, 0.625, ((2, 128),)),
        "connect": set_ends(jax.random.randint(seeds[7], (NCL, CLUSTERS), 0, EXT), jax.random.fold_in(seeds[7], 1), 0, EXT - 1).astype(jnp.int32),
        "recv_lower": set_ends(jax.random.randint(seeds[8], (GHOST * N_ROW * N_COL,), 0, NODE_DEV), jax.random.fold_in(seeds[8], 1), 0, NODE_DEV - 1).astype(jnp.int32),
        "recv_upper": set_ends(jax.random.randint(seeds[9], (GHOST * N_ROW * N_COL,), 0, NODE_DEV), jax.random.fold_in(seeds[9], 1), 0, NODE_DEV - 1).astype(jnp.int32),
    }


def reference(temp_thermal, send_index, interp_slot, interp_weight, disp, expansion, tangent, connect, recv_lower, recv_upper):
    devices = N_ROW * N_COL
    per_peer = RECV_DEV // devices
    table = send_index.reshape(devices, devices, per_peer)
    table = jnp.transpose(table, (1, 0, 2)) + (jnp.arange(devices, dtype=jnp.int32) * TN_DEV)[None, :, None]
    table = table.reshape(devices, RECV_DEV)

    def one_device(index):
        received = temp_thermal[:, table[index]]
        start = index * EXT
        slots = lax.dynamic_slice_in_dim(interp_slot, start, EXT, 1)
        weights = lax.dynamic_slice_in_dim(interp_weight, start, EXT, 1)
        picked = received[:, slots]
        temp_node = lax.optimization_barrier(jnp.sum(picked * weights[None], axis=1))
        strain = temp_node / jnp.sqrt(1.0 + temp_node * temp_node)
        local_disp = lax.dynamic_slice_in_dim(disp, start, EXT, 2).astype(jnp.float32)
        local_exp = lax.dynamic_slice_in_dim(expansion, start, EXT, 1)
        shifted = (local_disp - local_exp[:, None, :] * strain[None]).astype(jnp.bfloat16)
        blocks = lax.dynamic_slice_in_dim(tangent, index * CLU_DEV, CLU_DEV, 2)
        links = lax.dynamic_slice_in_dim(connect, index * CLU_DEV, CLU_DEV, 1)
        gathered = shifted[:, :, links]
        vectors = jnp.transpose(gathered, (0, 2, 1, 3)).reshape(3 * NCL, SCEN, CLU_DEV)
        products = jnp.einsum('ijc,jsc->isc', blocks.astype(jnp.float32), vectors.astype(jnp.float32))
        parts = jnp.transpose(products.reshape(3, NCL, SCEN, CLU_DEV), (0, 2, 1, 3))
        return jnp.zeros((3, SCEN, EXT), jnp.float32).at[:, :, links].add(parts)
    loads = lax.map(one_device, jnp.arange(devices, dtype=jnp.int32))
    owned = loads[:, :, :, :NODE_DEV]
    lower_rows = loads[:, :, :, NODE_DEV:NODE_DEV + GHOST]
    upper_rows = loads[:, :, :, NODE_DEV + GHOST:]
    column = jnp.arange(devices, dtype=jnp.int32) % N_COL
    zero_rows = jnp.zeros_like(upper_rows[:1])
    keep_low = (column > 0).astype(jnp.float32)[:, None, None, None]
    keep_high = (column < N_COL - 1).astype(jnp.float32)[:, None, None, None]
    from_lower = jnp.concatenate([zero_rows, upper_rows[:-1]], 0) * keep_low
    from_upper = jnp.concatenate([lower_rows[1:], zero_rows], 0) * keep_high
    lower_index = recv_lower.reshape(devices, GHOST)
    upper_index = recv_upper.reshape(devices, GHOST)

    def place(base, extra, where):
        return base.at[:, :, where].add(extra)
    result = jax.vmap(place)(owned, from_lower, lower_index)
    result = jax.vmap(place)(result, from_upper, upper_index)
    return jnp.transpose(result, (1, 2, 0, 3)).reshape(3, SCEN, NODE_DEV * devices)
```

```python
import functools

import jax
import jax.numpy as jnp
from jax import lax
from jax.experimental import pallas as pl
from jax.experimental.pallas import tpu as pltpu
from jax.sharding import PartitionSpec as P

F32 = jnp.float32
BF16 = jnp.bfloat16
I32 = jnp.int32
LANES = 128
WIDE = 256
AXES = ("row", "col")


def call(body, outs, scratch=()):
    return pl.pallas_call(
        body,
        out_shape=outs,
        scratch_shapes=scratch,
        compiler_params=pltpu.CompilerParams(vmem_limit_bytes=56 * 2**20),
    )


def split(x):
    high = x.astype(BF16)
    return high, (x - high.astype(F32)).astype(BF16)


def one_hot(low, iota):
    return jnp.where(iota == low.astype(F32).astype(BF16), jnp.ones((), BF16), jnp.zeros((), BF16))


def iota_of(columns):
    return lax.broadcasted_iota(I32, (WIDE, columns), 0).astype(F32).astype(BF16)


def choose(stacked, high, rows):
    out = stacked[0:rows]
    for h in range(1, stacked.shape[0] // rows):
        out = jnp.where(high == h, stacked[rows * h : rows * (h + 1)], out)
    return out


def swap_blocks(x):
    row = lax.broadcasted_iota(I32, x.shape, 0) >> 2
    col = lax.broadcasted_iota(I32, x.shape, 1) >> 5
    out = x
    for d in range(1, 4):
        moved = pltpu.roll(pltpu.roll(x, 16 - 4 * d, 0), 32 * d, 1)
        out = jnp.where(((col - row) & 3) == d, moved, out)
    return out


def fill_table(tab, read, blocks):
    for h in range(blocks):
        high, low = split(read(h))
        rows = high.shape[0]
        tab[h * rows : (h + 1) * rows, 0:WIDE] = high
        tab[h * rows : (h + 1) * rows, WIDE : 2 * WIDE] = low


def send_kernel(temp, index, out, tab):
    fill_table(tab, lambda h: temp[:, h * WIDE : (h + 1) * WIDE], temp.shape[1] // WIDE)
    iota = iota_of(WIDE)

    def body(j, _):
        idx = index[0:1, pl.ds(pl.multiple_of(j * WIDE, WIDE), WIDE)]
        hot = one_hot(idx & (WIDE - 1), iota)
        stacked = jnp.dot(tab[...], jnp.concatenate([hot, hot], 0), preferred_element_type=F32)
        got = choose(stacked, idx >> 8, 16)
        out[2 * j] = swap_blocks(got[:, 0:LANES])
        out[2 * j + 1] = swap_blocks(got[:, LANES:])
        return 0

    lax.fori_loop(0, index.shape[1] // WIDE, body, 0)


def main_kernel(arrived, slot, weight, disp, expansion, tangent, connect, prod, ghosts, tab, tab3, hot, vec, tf):
    extent = slot.shape[1]

    def table(h):
        return jnp.concatenate([swap_blocks(arrived[2 * h]), swap_blocks(arrived[2 * h + 1])], 1)

    fill_table(tab, table, arrived.shape[0] // 2)
    iota = iota_of(WIDE)

    def interpolate(j, _):
        js = pl.ds(pl.multiple_of(j * WIDE, WIDE), WIDE)
        temp = jnp.zeros((16, WIDE), F32)
        for c in range(4):
            idx = slot[pl.ds(c, 1), js]
            h2 = one_hot(idx & (WIDE - 1), iota)
            stacked = jnp.dot(tab[...], jnp.concatenate([h2, h2], 0), preferred_element_type=F32)
            temp = temp + weight[pl.ds(c, 1), js] * choose(stacked, idx >> 8, 16)
        strain = temp / jnp.sqrt(1.0 + temp * temp)
        for a in range(3):
            d = disp[16 * a : 16 * a + 16, js].astype(F32)
            s = (d - expansion[a : a + 1, js] * strain).astype(BF16)
            tab3[pl.ds(pl.multiple_of(j * 48 + a * 16, 16), 16), :] = s
        return 0

    lax.fori_loop(0, extent // WIDE, interpolate, 0)

    for p in range(16):
        idx = jnp.concatenate([connect[2 * p : 2 * p + 1, :], connect[2 * p + 1 : 2 * p + 2, :]], 1)
        h1 = one_hot(idx & (WIDE - 1), iota)
        hot[:, p * WIDE : (p + 1) * WIDE] = h1
        stacked = jnp.dot(tab3[...], h1, preferred_element_type=F32)
        got = choose(stacked, idx >> 8, 48)
        for a in range(3):
            vec[a * 32 + 2 * p] = got[16 * a : 16 * a + 16, 0:LANES]
            vec[a * 32 + 2 * p + 1] = got[16 * a : 16 * a + 16, LANES:]

    def widen(i, _):
        tf[pl.ds(pl.multiple_of(i * 96, 96), 96), :] = tangent[i].astype(F32)
        return 0

    lax.fori_loop(0, 96, widen, 0)
    group = 8

    def cluster(b, _):
        def inner(j8, sums):
            sums = list(sums)
            for jj in range(8):
                j = j8 * 8 + jj
                upper, lower = vec[j, 0:8, :], vec[j, 8:16, :]
                for i in range(group):
                    row = tf[pl.ds((b * group + i) * 96 + j, 1), :]
                    sums[2 * i] = sums[2 * i] + row * upper
                    sums[2 * i + 1] = sums[2 * i + 1] + row * lower
            return tuple(sums)

        sums = lax.fori_loop(0, 12, inner, tuple([jnp.zeros((8, LANES), F32)] * (2 * group)))
        a, m = b // 4, (b % 4) * group
        for i in range(group):
            cs = pl.ds(pl.multiple_of((m + i) * LANES, LANES), LANES)
            prod[pl.ds(pl.multiple_of(a * 16, 8), 8), cs] = sums[2 * i]
            prod[pl.ds(pl.multiple_of(a * 16 + 8, 8), 8), cs] = sums[2 * i + 1]
        return 0

    lax.fori_loop(0, 96 // group, cluster, 0)

    total = jnp.zeros((96, WIDE), F32)
    for p in range(16):
        idx = jnp.concatenate([connect[2 * p : 2 * p + 1, :], connect[2 * p + 1 : 2 * p + 2, :]], 1)
        x = jnp.where((idx >> 8) == 16, prod[:, p * WIDE : (p + 1) * WIDE], 0.0)
        total = total + lax.dot_general(
            jnp.concatenate(split(x), 0),
            hot[:, p * WIDE : (p + 1) * WIDE],
            (((1,), (1,)), ((), ())),
            preferred_element_type=F32,
        )
    ghosts[...] = total[0:48] + total[48:96]


def spread(values, high, hot_t, blocks):
    rows = []
    for part in split(values):
        wide = part.astype(F32)
        rows += [jnp.where(high == h, wide, 0.0).astype(BF16) for h in range(blocks)]
    both = lax.dot_general(
        jnp.concatenate(rows, 0), hot_t, (((1,), (1,)), ((), ())), preferred_element_type=F32
    )
    half = blocks * 48
    return both[0:half] + both[half:]


def owned_kernel(prod, connect, out, a_scr, hot):
    blocks = out.shape[1] // WIDE
    half = blocks * 48
    iota = iota_of(WIDE)
    for p in range(16):
        ks = slice(p * WIDE, (p + 1) * WIDE)
        idx = jnp.concatenate([connect[2 * p : 2 * p + 1, :], connect[2 * p + 1 : 2 * p + 2, :]], 1)
        hot[:, ks] = one_hot(idx & (WIDE - 1), iota)
        high, low = split(prod[:, ks])
        high, low = high.astype(F32), low.astype(F32)
        for h in range(blocks):
            mask = (idx >> 8) == h
            a_scr[h * 48 : (h + 1) * 48, ks] = jnp.where(mask, high, 0.0).astype(BF16)
            a_scr[half + h * 48 : half + (h + 1) * 48, ks] = jnp.where(mask, low, 0.0).astype(BF16)
    dims = (((1,), (1,)), ((), ()))
    total = lax.dot_general(a_scr[0:half], hot[...], dims, preferred_element_type=F32)
    total = total + lax.dot_general(a_scr[half:], hot[...], dims, preferred_element_type=F32)
    for h in range(blocks):
        out[:, h * WIDE : (h + 1) * WIDE] = total[48 * h : 48 * h + 48]


def ghost_kernel(own, from_lower, from_upper, lower, upper, out):
    blocks = out.shape[1] // WIDE
    idx = jnp.concatenate([lower[...], upper[...]], 1)
    hot = one_hot(idx & (WIDE - 1), iota_of(WIDE))
    total = spread(jnp.concatenate([from_lower[...], from_upper[...]], 1), idx >> 8, hot, blocks)
    for h in range(blocks):
        hs = slice(h * WIDE, (h + 1) * WIDE)
        out[:, hs] = own[:, hs] + total[48 * h : 48 * h + 48]


def neighbour(block, distance):
    devices = range(lax.axis_size("col"))
    route = [(i - distance, i) for i in devices if i - distance in devices]
    return lax.ppermute(block, "col", route)


def shards(temp_thermal, send_index, interp_slot, interp_weight, disp, expansion, tangent, connect, recv_lower, recv_upper):
    shape = jax.ShapeDtypeStruct
    packed = call(
        send_kernel, shape((32, 16, LANES), F32), [pltpu.VMEM((256, 2 * WIDE), BF16)]
    )(temp_thermal, send_index)
    arrived = lax.all_to_all(packed.reshape(128, 4, LANES), AXES, split_axis=0, concat_axis=0, tiled=True)
    arrived = arrived.reshape(32, 16, LANES)
    prod, ghosts = call(
        main_kernel,
        (shape((48, 4096), F32), shape((48, WIDE), F32)),
        [
            pltpu.VMEM((256, 2 * WIDE), BF16),
            pltpu.VMEM((17 * 48, WIDE), BF16),
            pltpu.VMEM((WIDE, 4096), BF16),
            pltpu.VMEM((96, 16, LANES), F32),
            pltpu.VMEM((96 * 96, LANES), F32),
        ],
    )(arrived, interp_slot, interp_weight, disp.reshape(48, -1), expansion, tangent, connect)
    from_lower = neighbour(ghosts[:, LANES:], 1)
    from_upper = neighbour(ghosts[:, :LANES], -1)
    own = call(
        owned_kernel,
        shape((48, 4096), F32),
        [pltpu.VMEM((2 * 16 * 48, 4096), BF16), pltpu.VMEM((WIDE, 4096), BF16)],
    )(prod, connect)
    result = call(ghost_kernel, shape((48, 4096), F32))(
        own, from_lower, from_upper, recv_lower.reshape(1, LANES), recv_upper.reshape(1, LANES)
    )
    return result.reshape(3, 16, 4096)


def solution(mesh):
    in_specs = (
        P(None, AXES),
        P(AXES, None),
        P(None, AXES),
        P(None, AXES),
        P(None, None, AXES),
        P(None, AXES),
        P(None, None, AXES),
        P(None, AXES),
        P(AXES),
        P(AXES),
    )
    out_specs = P(None, None, AXES)
    return jax.shard_map(shards, mesh=mesh, in_specs=in_specs, out_specs=out_specs, check_vma=False)
```

```python
import jax
import jax.numpy as jnp
from jax import lax
from jax.experimental import pallas as pl
from jax.experimental.pallas import tpu as pltpu
from jax.sharding import PartitionSpec as P

F32 = jnp.float32
BF16 = jnp.bfloat16
I32 = jnp.int32
LANES = 128
WIDE = 256
AXES = ("row", "col")
NT = (((1,), (1,)), ((), ()))
VMEM_BYTES = 32 * 2**20


def call(body, outs, scratch=()):
    return pl.pallas_call(
        body,
        out_shape=outs,
        scratch_shapes=scratch,
        compiler_params=pltpu.CompilerParams(vmem_limit_bytes=VMEM_BYTES),
    )


def split(x):
    high = x.astype(BF16)
    return high, (x - high.astype(F32)).astype(BF16)


def one_hot(low, iota):
    return jnp.where(iota == low.astype(F32).astype(BF16), jnp.ones((), BF16), jnp.zeros((), BF16))


def iota_of(columns):
    return lax.broadcasted_iota(I32, (WIDE, columns), 0).astype(F32).astype(BF16)


def choose(stacked, high, rows):
    out = stacked[0:rows]
    for h in range(1, stacked.shape[0] // rows):
        out = jnp.where(high == h, stacked[rows * h : rows * (h + 1)], out)
    return out


def swap_blocks(x):
    row = lax.broadcasted_iota(I32, x.shape, 0) >> 2
    col = lax.broadcasted_iota(I32, x.shape, 1) >> 5
    out = x
    for d in range(1, 4):
        moved = pltpu.roll(pltpu.roll(x, 16 - 4 * d, 0), 32 * d, 1)
        out = jnp.where(((col - row) & 3) == d, moved, out)
    return out


def fill_table(tab, read, blocks):
    for h in range(blocks):
        high, low = split(read(h))
        rows = high.shape[0]
        tab[h * rows : (h + 1) * rows, 0:WIDE] = high
        tab[h * rows : (h + 1) * rows, WIDE : 2 * WIDE] = low


def send_kernel(temp, index, out, tab):
    fill_table(tab, lambda h: temp[:, h * WIDE : (h + 1) * WIDE], temp.shape[1] // WIDE)
    iota = iota_of(WIDE)
    for j in range(index.shape[1] // WIDE):
        idx = index[0:1, j * WIDE : (j + 1) * WIDE]
        hot = one_hot(idx & (WIDE - 1), iota)
        stacked = jnp.dot(tab[...], jnp.concatenate([hot, hot], 0), preferred_element_type=F32)
        got = choose(stacked, idx >> 8, 16)
        out[2 * j] = swap_blocks(got[:, 0:LANES])
        out[2 * j + 1] = swap_blocks(got[:, LANES:])


def main_kernel(arrived, slot, weight, disp, expansion, blocks, connect, prod, lower, upper, tab, tab3, matrices, sem):
    fetch = pltpu.make_async_copy(blocks, matrices, sem)
    fetch.start()
    extent = slot.shape[1]

    def table(h):
        return jnp.concatenate([swap_blocks(arrived[2 * h]), swap_blocks(arrived[2 * h + 1])], 1)

    fill_table(tab, table, arrived.shape[0] // 2)
    iota = iota_of(WIDE)

    for j in range(extent // WIDE):
        js = slice(j * WIDE, (j + 1) * WIDE)
        temp = jnp.zeros((16, WIDE), F32)
        for c in range(4):
            idx = slot[c : c + 1, js]
            hot = one_hot(idx & (WIDE - 1), iota)
            stacked = jnp.dot(tab[...], jnp.concatenate([hot, hot], 0), preferred_element_type=F32)
            temp = temp + weight[c : c + 1, js] * choose(stacked, idx >> 8, 16)
        strain = temp / jnp.sqrt(1.0 + temp * temp)
        for a in range(3):
            d = disp[16 * a : 16 * a + 16, js].astype(F32)
            s = (d - expansion[a : a + 1, js] * strain).astype(BF16)
            tab3[j * 48 + a * 16 : j * 48 + a * 16 + 16, :] = s

    fetch.wait()
    lane = lax.broadcasted_iota(I32, (16, LANES), 1) >> 5
    total = jnp.zeros((48, WIDE), F32)
    for p in range(connect.shape[1] // WIDE):
        idx = connect[0:1, p * WIDE : (p + 1) * WIDE]
        hot = one_hot(idx & (WIDE - 1), iota)
        got = choose(jnp.dot(tab3[...], hot, preferred_element_type=F32), idx >> 8, 48)
        pieces = []
        for half in range(2):
            x = [got[16 * a : 16 * a + 16, half * LANES : (half + 1) * LANES] for a in range(3)]
            y = []
            for u in range(4):
                v = [turn(x[a], a - u) for a in range(3)]
                v = jnp.where(lane == 0, v[0], jnp.where(lane == 1, v[1], v[2])).astype(BF16)
                one = jnp.dot(v[:, 0:96], matrices[p * 8 + half * 4 + u], preferred_element_type=F32)
                y.append(jnp.concatenate([one, jnp.zeros((16, 32), F32)], 1))
            rows = []
            for a in range(3):
                w = [turn(y[u], u - a) for u in range(4)]
                rows.append(jnp.where(lane == 0, w[0], jnp.where(lane == 1, w[1], jnp.where(lane == 2, w[2], w[3]))))
            pieces.append(jnp.concatenate(rows, 0))
        value = jnp.concatenate(pieces, 1)
        prod[:, p * WIDE : (p + 1) * WIDE] = value
        high, low = split(jnp.where((idx >> 8) == extent // WIDE - 1, value, 0.0))
        total = total + lax.dot_general(
            jnp.concatenate([high, low], 1), jnp.concatenate([hot, hot], 1), NT, preferred_element_type=F32
        )
    lower[...] = total[:, 0:LANES]
    upper[...] = total[:, LANES:]


def turn(x, blocks):
    return pltpu.roll(x, (32 * blocks) % LANES, 1) if blocks else x


def final_kernel(prod, connect, from_lower, from_upper, at_lower, at_upper, out):
    blocks = out.shape[1] // WIDE
    iota = iota_of(WIDE)
    zero = jnp.zeros((), BF16)

    def spread(x, idx):
        hot = one_hot(idx & (WIDE - 1), iota)
        high = jnp.broadcast_to((idx >> 8).astype(F32).astype(BF16), x.shape)
        sides = [
            jnp.concatenate([jnp.where(high == jnp.array(h, BF16), part, zero) for h in range(blocks)], 0)
            for part in split(x)
        ]
        return lax.dot_general(
            jnp.concatenate(sides, 1), jnp.concatenate([hot, hot], 1), NT, preferred_element_type=F32
        )

    total = None
    for p in range(connect.shape[1] // WIDE):
        ks = slice(p * WIDE, (p + 1) * WIDE)
        term = spread(prod[:, ks], connect[0:1, ks])
        total = term if total is None else total + term
    ghosts = jnp.concatenate([from_lower[...], from_upper[...]], 1)
    total = total + spread(ghosts, jnp.concatenate([at_lower[...], at_upper[...]], 1))
    for h in range(blocks):
        out[:, h * WIDE : (h + 1) * WIDE] = total[48 * h : 48 * h + 48]


def neighbour(block, distance):
    devices = range(lax.axis_size("col"))
    route = [(i - distance, i) for i in devices if i - distance in devices]
    return lax.ppermute(block, "col", route)


def main_call(*args):
    shape = jax.ShapeDtypeStruct
    whole = pl.BlockSpec(memory_space=pltpu.VMEM)
    return pl.pallas_call(
        main_kernel,
        out_shape=(shape((48, 4096), F32), shape((48, LANES), F32), shape((48, LANES), F32)),
        in_specs=[whole] * 5 + [pl.BlockSpec(memory_space=pl.ANY), whole],
        out_specs=(whole, whole, whole),
        scratch_shapes=[
            pltpu.VMEM((256, 2 * WIDE), BF16),
            pltpu.VMEM((17 * 48, WIDE), BF16),
            pltpu.VMEM((128, 96, 96), BF16),
            pltpu.SemaphoreType.DMA(()),
        ],
        compiler_params=pltpu.CompilerParams(vmem_limit_bytes=VMEM_BYTES),
    )(*args)


def shards(temp_thermal, send_index, interp_slot, interp_weight, disp, expansion, tangent, connect, recv_lower, recv_upper):
    shape = jax.ShapeDtypeStruct
    packed = call(
        send_kernel, shape((32, 16, LANES), F32), [pltpu.VMEM((256, 2 * WIDE), BF16)]
    )(temp_thermal, send_index)
    arrived = lax.all_to_all(packed.reshape(128, 4, LANES), AXES, split_axis=0, concat_axis=0, tiled=True)
    arrived = arrived.reshape(32, 16, LANES)
    links = connect.T.reshape(1, 4096)
    blocks = jnp.transpose(tangent, (2, 1, 0))
    prod, lower, upper = main_call(arrived, interp_slot, interp_weight, disp.reshape(48, -1), expansion, blocks, links)
    from_lower = neighbour(upper, 1)
    from_upper = neighbour(lower, -1)
    result = call(final_kernel, shape((48, 4096), F32))(
        prod, links, from_lower, from_upper, recv_lower.reshape(1, LANES), recv_upper.reshape(1, LANES)
    )
    return result.reshape(3, 16, 4096)


def solution(mesh):
    in_specs = (
        P(None, AXES),
        P(AXES, None),
        P(None, AXES),
        P(None, AXES),
        P(None, None, AXES),
        P(None, AXES),
        P(None, None, AXES),
        P(None, AXES),
        P(AXES),
        P(AXES),
    )
    out_specs = P(None, None, AXES)
    return jax.shard_map(shards, mesh=mesh, in_specs=in_specs, out_specs=out_specs, check_vma=False)
```

```python
import jax
import jax.numpy as jnp
from jax import lax
from jax.experimental import pallas as pl
from jax.experimental.pallas import tpu as pltpu
from jax.sharding import PartitionSpec as P

F32 = jnp.float32
BF16 = jnp.bfloat16
I32 = jnp.int32
LANES = 128
WIDE = 256
AXES = ("row", "col")
NT = (((1,), (1,)), ((), ()))
VMEM_BYTES = 32 * 2**20


def split(x):
    high = x.astype(BF16)
    return high, (x - high.astype(F32)).astype(BF16)


def one_hot(low, iota):
    return jnp.where(iota == low.astype(F32).astype(BF16), jnp.ones((), BF16), jnp.zeros((), BF16))


def iota_of(columns):
    return lax.broadcasted_iota(I32, (WIDE, columns), 0).astype(F32).astype(BF16)


def choose(stacked, high, rows):
    out = stacked[0:rows]
    for h in range(1, stacked.shape[0] // rows):
        out = jnp.where(high == h, stacked[rows * h : rows * (h + 1)], out)
    return out


def swap_blocks(x):
    row = lax.broadcasted_iota(I32, x.shape, 0) >> 2
    col = lax.broadcasted_iota(I32, x.shape, 1) >> 5
    out = x
    for d in range(1, 4):
        moved = pltpu.roll(pltpu.roll(x, 16 - 4 * d, 0), 32 * d, 1)
        out = jnp.where(((col - row) & 3) == d, moved, out)
    return out


def fill_block(tab, h, block):
    rows = block.shape[0]
    high, low = split(block)
    tab[h * rows : (h + 1) * rows, 0:WIDE] = high
    tab[h * rows : (h + 1) * rows, WIDE : 2 * WIDE] = low


def send_kernel(temp_hbm, index_hbm, out, tab, temp, index, sems):
    parts = 4
    width = temp.shape[1] // parts
    copies = [
        pltpu.make_async_copy(temp_hbm.at[:, pl.ds(i * width, width)], temp.at[:, pl.ds(i * width, width)], sems.at[i])
        for i in range(parts)
    ]
    copies.append(pltpu.make_async_copy(index_hbm, index, sems.at[parts]))
    for copy in copies:
        copy.start()
    iota = iota_of(WIDE)
    for h in range(temp.shape[1] // WIDE):
        if h * WIDE % width == 0:
            copies[h * WIDE // width].wait()
        fill_block(tab, h, temp[:, h * WIDE : (h + 1) * WIDE])
    copies[parts].wait()
    for j in range(index.shape[1] // WIDE):
        idx = index[0:1, j * WIDE : (j + 1) * WIDE]
        hot = one_hot(idx & (WIDE - 1), iota)
        stacked = jnp.dot(tab[...], jnp.concatenate([hot, hot], 0), preferred_element_type=F32)
        got = choose(stacked, idx >> 8, 16)
        out[2 * j] = swap_blocks(got[:, 0:LANES])
        out[2 * j + 1] = swap_blocks(got[:, LANES:])


def main_kernel(
    arrived, slot_hbm, weight_hbm, disp_hbm, expansion_hbm, blocks, connect,
    prod, lower, upper,
    tab, tab3, slot, weight, disp, expansion, matrices, sems,
):
    pairs = ((slot_hbm, slot), (weight_hbm, weight), (expansion_hbm, expansion), (disp_hbm, disp), (blocks, matrices))
    copies = [pltpu.make_async_copy(source, place, sems.at[i]) for i, (source, place) in enumerate(pairs)]
    for copy in copies:
        copy.start()
    extent = slot.shape[1]

    for h in range(arrived.shape[0] // 2):
        fill_block(tab, h, jnp.concatenate([swap_blocks(arrived[2 * h]), swap_blocks(arrived[2 * h + 1])], 1))
    iota = iota_of(WIDE)
    for copy in copies[0:4]:
        copy.wait()

    for j in range(extent // WIDE):
        js = slice(j * WIDE, (j + 1) * WIDE)
        temp = jnp.zeros((16, WIDE), F32)
        for c in range(4):
            idx = slot[c : c + 1, js]
            hot = one_hot(idx & (WIDE - 1), iota)
            stacked = jnp.dot(tab[...], jnp.concatenate([hot, hot], 0), preferred_element_type=F32)
            temp = temp + weight[c : c + 1, js] * choose(stacked, idx >> 8, 16)
        strain = temp / jnp.sqrt(1.0 + temp * temp)
        for a in range(3):
            d = disp[16 * a : 16 * a + 16, js].astype(F32)
            s = (d - expansion[a : a + 1, js] * strain).astype(BF16)
            tab3[j * 48 + a * 16 : j * 48 + a * 16 + 16, :] = s

    copies[4].wait()
    lane = lax.broadcasted_iota(I32, (16, LANES), 1) >> 5
    total = jnp.zeros((48, WIDE), F32)
    for p in range(connect.shape[1] // WIDE):
        idx = connect[0:1, p * WIDE : (p + 1) * WIDE]
        hot = one_hot(idx & (WIDE - 1), iota)
        got = choose(jnp.dot(tab3[...], hot, preferred_element_type=F32), idx >> 8, 48)
        pieces = []
        for half in range(2):
            x = [got[16 * a : 16 * a + 16, half * LANES : (half + 1) * LANES] for a in range(3)]
            y = []
            for u in range(4):
                v = [turn(x[a], a - u) for a in range(3)]
                v = jnp.where(lane == 0, v[0], jnp.where(lane == 1, v[1], v[2])).astype(BF16)
                one = jnp.dot(v[:, 0:96], matrices[p * 8 + half * 4 + u], preferred_element_type=F32)
                y.append(jnp.concatenate([one, jnp.zeros((16, 32), F32)], 1))
            rows = []
            for a in range(3):
                w = [turn(y[u], u - a) for u in range(4)]
                rows.append(jnp.where(lane == 0, w[0], jnp.where(lane == 1, w[1], jnp.where(lane == 2, w[2], w[3]))))
            pieces.append(jnp.concatenate(rows, 0))
        value = jnp.concatenate(pieces, 1)
        prod[:, p * WIDE : (p + 1) * WIDE] = value
        high, low = split(jnp.where((idx >> 8) == extent // WIDE - 1, value, 0.0))
        total = total + lax.dot_general(
            jnp.concatenate([high, low], 1), jnp.concatenate([hot, hot], 1), NT, preferred_element_type=F32
        )
    lower[...] = total[:, 0:LANES]
    upper[...] = total[:, LANES:]


def turn(x, blocks):
    return pltpu.roll(x, (32 * blocks) % LANES, 1) if blocks else x


def spread(x, idx, blocks):
    zero = jnp.zeros((), BF16)
    hot = one_hot(idx & (WIDE - 1), iota_of(WIDE))
    high = jnp.broadcast_to((idx >> 8).astype(F32).astype(BF16), x.shape)
    sides = [
        jnp.concatenate([jnp.where(high == jnp.array(h, BF16), part, zero) for h in range(blocks)], 0)
        for part in split(x)
    ]
    return lax.dot_general(
        jnp.concatenate(sides, 1), jnp.concatenate([hot, hot], 1), NT, preferred_element_type=F32
    )


def owned_kernel(prod, connect, out):
    blocks = out.shape[1] // WIDE
    total = None
    for p in range(connect.shape[1] // WIDE):
        ks = slice(p * WIDE, (p + 1) * WIDE)
        term = spread(prod[:, ks], connect[0:1, ks], blocks)
        total = term if total is None else total + term
    for h in range(blocks):
        out[:, h * WIDE : (h + 1) * WIDE] = total[48 * h : 48 * h + 48]


def ghost_kernel(own, from_lower, from_upper, at, out):
    blocks = out.shape[1] // WIDE
    total = spread(jnp.concatenate([from_lower[...], from_upper[...]], 1), at[...], blocks)
    for h in range(blocks):
        hs = slice(h * WIDE, (h + 1) * WIDE)
        out[:, hs] = own[:, hs] + total[48 * h : 48 * h + 48]


def neighbour(block, distance):
    count = lax.axis_size("col")
    return lax.ppermute(block, "col", [(i, (i + distance) % count) for i in range(count)])


def shards(temp_thermal, send_index, interp_slot, interp_weight, disp, expansion, tangent, connect, recv_lower, recv_upper):
    shape = jax.ShapeDtypeStruct
    here = pl.BlockSpec(memory_space=pltpu.VMEM)
    away = pl.BlockSpec(memory_space=pltpu.HBM)
    free = pl.BlockSpec(memory_space=pl.ANY)
    keep = lambda x: pltpu.with_memory_space_constraint(x, pltpu.HBM)
    params = pltpu.CompilerParams(vmem_limit_bytes=VMEM_BYTES)
    packed = pl.pallas_call(
        send_kernel,
        out_shape=shape((32, 16, LANES), F32),
        in_specs=[away, away],
        out_specs=here,
        scratch_shapes=[
            pltpu.VMEM((256, 2 * WIDE), BF16),
            pltpu.VMEM((16, 4096), F32),
            pltpu.VMEM((1, 4096), I32),
            pltpu.SemaphoreType.DMA((5,)),
        ],
        compiler_params=params,
    )(keep(temp_thermal), keep(send_index))
    arrived = lax.all_to_all(packed.reshape(128, 4, LANES), AXES, split_axis=0, concat_axis=0, tiled=True)
    arrived = arrived.reshape(32, 16, LANES)
    links = connect.T.reshape(1, 4096)
    blocks = jnp.transpose(tangent, (2, 1, 0))
    col = lax.axis_index("col")
    at = jnp.concatenate(
        [jnp.where(col > 0, recv_lower, -1), jnp.where(col < lax.axis_size("col") - 1, recv_upper, -1)]
    ).reshape(1, WIDE)
    prod, lower, upper = pl.pallas_call(
        main_kernel,
        out_shape=(shape((48, 4096), F32), shape((48, LANES), F32), shape((48, LANES), F32)),
        in_specs=[here, away, away, away, away, free, here],
        out_specs=(here, here, here),
        scratch_shapes=[
            pltpu.VMEM((256, 2 * WIDE), BF16),
            pltpu.VMEM((17 * 48, WIDE), BF16),
            pltpu.VMEM((4, 4352), I32),
            pltpu.VMEM((4, 4352), F32),
            pltpu.VMEM((48, 4352), BF16),
            pltpu.VMEM((3, 4352), F32),
            pltpu.VMEM((128, 96, 96), BF16),
            pltpu.SemaphoreType.DMA((5,)),
        ],
        compiler_params=params,
    )(
        arrived, keep(interp_slot), keep(interp_weight), keep(disp.reshape(48, -1)), keep(expansion), blocks, links
    )
    from_lower = neighbour(upper, 1)
    from_upper = neighbour(lower, -1)
    own = pl.pallas_call(owned_kernel, out_shape=shape((48, 4096), F32), compiler_params=params)(prod, links)
    result = pl.pallas_call(ghost_kernel, out_shape=shape((48, 4096), F32), compiler_params=params)(
        own, from_lower, from_upper, at
    )
    return result.reshape(3, 16, 4096)


def solution(mesh):
    in_specs = (
        P(None, AXES),
        P(AXES, None),
        P(None, AXES),
        P(None, AXES),
        P(None, None, AXES),
        P(None, AXES),
        P(None, None, AXES),
        P(None, AXES),
        P(AXES),
        P(AXES),
    )
    out_specs = P(None, None, AXES)
    return jax.shard_map(shards, mesh=mesh, in_specs=in_specs, out_specs=out_specs, check_vma=False)
```

```python
import jax
import jax.numpy as jnp
from jax import lax
from jax.experimental import pallas as pl
from jax.experimental.pallas import tpu as pltpu
from jax.sharding import PartitionSpec as P

F32 = jnp.float32
BF16 = jnp.bfloat16
I32 = jnp.int32
LANES = 128
WIDE = 256
AXES = ("row", "col")
NT = (((1,), (1,)), ((), ()))
VMEM_BYTES = 32 * 2**20


def split(x):
    high = x.astype(BF16)
    return high, (x - high.astype(F32)).astype(BF16)


def one_hot(low, iota):
    return jnp.where(iota == low.astype(F32).astype(BF16), jnp.ones((), BF16), jnp.zeros((), BF16))


def iota_of(columns):
    return lax.broadcasted_iota(I32, (WIDE, columns), 0).astype(F32).astype(BF16)


def choose(stacked, high, rows):
    out = stacked[0:rows]
    for h in range(1, stacked.shape[0] // rows):
        out = jnp.where(high == h, stacked[rows * h : rows * (h + 1)], out)
    return out


def swap_blocks(x):
    row = lax.broadcasted_iota(I32, x.shape, 0) >> 2
    col = lax.broadcasted_iota(I32, x.shape, 1) >> 5
    out = x
    for d in range(1, 4):
        moved = pltpu.roll(pltpu.roll(x, 16 - 4 * d, 0), 32 * d, 1)
        out = jnp.where(((col - row) & 3) == d, moved, out)
    return out


def fill_block(tab, h, block):
    rows = block.shape[0]
    high, low = split(block)
    tab[h * rows : (h + 1) * rows, 0:WIDE] = high
    tab[h * rows : (h + 1) * rows, WIDE : 2 * WIDE] = low


def send_kernel(temp_hbm, index_hbm, out, tab, temp, index, sems):
    parts = 4
    width = temp.shape[1] // parts
    copies = [
        pltpu.make_async_copy(temp_hbm.at[:, pl.ds(i * width, width)], temp.at[:, pl.ds(i * width, width)], sems.at[i])
        for i in range(parts)
    ]
    copies.append(pltpu.make_async_copy(index_hbm, index, sems.at[parts]))
    for copy in copies:
        copy.start()
    iota = iota_of(WIDE)
    for h in range(temp.shape[1] // WIDE):
        if h * WIDE % width == 0:
            copies[h * WIDE // width].wait()
        fill_block(tab, h, temp[:, h * WIDE : (h + 1) * WIDE])
    copies[parts].wait()
    for j in range(index.shape[1] // WIDE):
        idx = index[0:1, j * WIDE : (j + 1) * WIDE]
        hot = one_hot(idx & (WIDE - 1), iota)
        stacked = jnp.dot(tab[...], jnp.concatenate([hot, hot], 0), preferred_element_type=F32)
        got = choose(stacked, idx >> 8, 16)
        out[2 * j] = swap_blocks(got[:, 0:LANES])
        out[2 * j + 1] = swap_blocks(got[:, LANES:])


def main_kernel(
    arrived, slot_hbm, weight_hbm, disp_hbm, expansion_hbm, blocks, connect,
    prod, lower, upper,
    tab, tab3, slot, weight, disp, expansion, matrices, vec, sems,
):
    pairs = ((slot_hbm, slot), (weight_hbm, weight), (expansion_hbm, expansion), (disp_hbm, disp), (blocks, matrices))
    copies = [pltpu.make_async_copy(source, place, sems.at[i]) for i, (source, place) in enumerate(pairs)]
    for copy in copies:
        copy.start()
    extent = slot.shape[1]

    for h in range(arrived.shape[0] // 2):
        fill_block(tab, h, jnp.concatenate([swap_blocks(arrived[2 * h]), swap_blocks(arrived[2 * h + 1])], 1))
    iota = iota_of(WIDE)
    for copy in copies[0:4]:
        copy.wait()

    for j in range(extent // WIDE):
        js = slice(j * WIDE, (j + 1) * WIDE)
        temp = jnp.zeros((16, WIDE), F32)
        for c in range(4):
            idx = slot[c : c + 1, js]
            hot = one_hot(idx & (WIDE - 1), iota)
            stacked = jnp.dot(tab[...], jnp.concatenate([hot, hot], 0), preferred_element_type=F32)
            temp = temp + weight[c : c + 1, js] * choose(stacked, idx >> 8, 16)
        strain = temp / jnp.sqrt(1.0 + temp * temp)
        for a in range(3):
            d = disp[16 * a : 16 * a + 16, js].astype(F32)
            s = (d - expansion[a : a + 1, js] * strain).astype(BF16)
            tab3[j * 48 + a * 16 : j * 48 + a * 16 + 16, :] = s

    copies[4].wait()
    lane = lax.broadcasted_iota(I32, (16, LANES), 1) >> 5
    count = connect.shape[1] // WIDE

    def indices(p):
        return connect[0:1, p * WIDE : (p + 1) * WIDE]

    def gather(p):
        idx = indices(p)
        hot = one_hot(idx & (WIDE - 1), iota)
        return choose(jnp.dot(tab3[...], hot, preferred_element_type=F32), idx >> 8, 48)

    def multiply(p, got):
        pieces = []
        for half in range(2):
            x = [got[16 * a : 16 * a + 16, half * LANES : (half + 1) * LANES] for a in range(3)]
            y = []
            for u in range(4):
                v = [turn(x[a], a - u) for a in range(3)]
                v = jnp.where(lane == 0, v[0], jnp.where(lane == 1, v[1], v[2])).astype(BF16)
                one = jnp.dot(v[:, 0:96], matrices[p * 8 + half * 4 + u], preferred_element_type=F32)
                y.append(jnp.concatenate([one, jnp.zeros((16, 32), F32)], 1))
            rows = []
            for a in range(3):
                w = [turn(y[u], u - a) for u in range(4)]
                rows.append(jnp.where(lane == 0, w[0], jnp.where(lane == 1, w[1], jnp.where(lane == 2, w[2], w[3]))))
            pieces.append(jnp.concatenate(rows, 0))
        value = jnp.concatenate(pieces, 1)
        prod[:, p * WIDE : (p + 1) * WIDE] = value

    def ghosts(p, total):
        idx = indices(p)
        hot = one_hot(idx & (WIDE - 1), iota)
        value = prod[:, p * WIDE : (p + 1) * WIDE]
        high, low = split(jnp.where((idx >> 8) == extent // WIDE - 1, value, 0.0))
        return total + lax.dot_general(jnp.concatenate([high, low], 0), hot, NT, preferred_element_type=F32)

    total = jnp.zeros((96, WIDE), F32)
    for p in range(count):
        vec[:, p * WIDE : (p + 1) * WIDE] = gather(p)
    for p in range(count):
        multiply(p, vec[:, p * WIDE : (p + 1) * WIDE])
    for p in range(count):
        total = ghosts(p, total)
    total = total[0:48] + total[48:96]
    lower[...] = total[:, 0:LANES]
    upper[...] = total[:, LANES:]


def turn(x, blocks):
    return pltpu.roll(x, (32 * blocks) % LANES, 1) if blocks else x


def spread(x, idx, blocks):
    zero = jnp.zeros((), BF16)
    hot = one_hot(idx & (WIDE - 1), iota_of(WIDE))
    high = jnp.broadcast_to((idx >> 8).astype(F32).astype(BF16), x.shape)
    sides = [
        jnp.concatenate([jnp.where(high == jnp.array(h, BF16), part, zero) for h in range(blocks)], 0)
        for part in split(x)
    ]
    return lax.dot_general(
        jnp.concatenate(sides, 1), jnp.concatenate([hot, hot], 1), NT, preferred_element_type=F32
    )


def owned_kernel(prod, connect, out):
    blocks = out.shape[1] // WIDE
    total = None
    for p in range(connect.shape[1] // WIDE):
        ks = slice(p * WIDE, (p + 1) * WIDE)
        term = spread(prod[:, ks], connect[0:1, ks], blocks)
        total = term if total is None else total + term
    for h in range(blocks):
        out[:, h * WIDE : (h + 1) * WIDE] = total[48 * h : 48 * h + 48]


def ghost_kernel(own, from_lower, from_upper, at, out):
    blocks = out.shape[1] // WIDE
    total = spread(jnp.concatenate([from_lower[...], from_upper[...]], 1), at[...], blocks)
    for h in range(blocks):
        hs = slice(h * WIDE, (h + 1) * WIDE)
        out[:, hs] = own[:, hs] + total[48 * h : 48 * h + 48]


def neighbour(block, distance):
    count = lax.axis_size("col")
    return lax.ppermute(block, "col", [(i, (i + distance) % count) for i in range(count)])


def shards(temp_thermal, send_index, interp_slot, interp_weight, disp, expansion, tangent, connect, recv_lower, recv_upper):
    shape = jax.ShapeDtypeStruct
    here = pl.BlockSpec(memory_space=pltpu.VMEM)
    away = pl.BlockSpec(memory_space=pltpu.HBM)
    free = pl.BlockSpec(memory_space=pl.ANY)
    keep = lambda x: pltpu.with_memory_space_constraint(x, pltpu.HBM)
    params = pltpu.CompilerParams(vmem_limit_bytes=VMEM_BYTES)
    packed = pl.pallas_call(
        send_kernel,
        out_shape=shape((32, 16, LANES), F32),
        in_specs=[away, away],
        out_specs=here,
        scratch_shapes=[
            pltpu.VMEM((256, 2 * WIDE), BF16),
            pltpu.VMEM((16, 4096), F32),
            pltpu.VMEM((1, 4096), I32),
            pltpu.SemaphoreType.DMA((5,)),
        ],
        compiler_params=params,
    )(keep(temp_thermal), keep(send_index))
    arrived = lax.all_to_all(packed.reshape(128, 4, LANES), AXES, split_axis=0, concat_axis=0, tiled=True)
    arrived = arrived.reshape(32, 16, LANES)
    links = connect.T.reshape(1, 4096)
    blocks = jnp.transpose(tangent, (2, 1, 0))
    col = lax.axis_index("col")
    at = jnp.concatenate(
        [jnp.where(col > 0, recv_lower, -1), jnp.where(col < lax.axis_size("col") - 1, recv_upper, -1)]
    ).reshape(1, WIDE)
    prod, lower, upper = pl.pallas_call(
        main_kernel,
        out_shape=(shape((48, 4096), F32), shape((48, LANES), F32), shape((48, LANES), F32)),
        in_specs=[here, away, away, away, away, free, here],
        out_specs=(here, here, here),
        scratch_shapes=[
            pltpu.VMEM((256, 2 * WIDE), BF16),
            pltpu.VMEM((17 * 48, WIDE), BF16),
            pltpu.VMEM((4, 4352), I32),
            pltpu.VMEM((4, 4352), F32),
            pltpu.VMEM((48, 4352), BF16),
            pltpu.VMEM((3, 4352), F32),
            pltpu.VMEM((128, 96, 96), BF16),
            pltpu.VMEM((48, 4096), F32),
            pltpu.SemaphoreType.DMA((5,)),
        ],
        compiler_params=params,
    )(
        arrived, keep(interp_slot), keep(interp_weight), keep(disp.reshape(48, -1)), keep(expansion), blocks, links
    )
    from_lower = neighbour(upper, 1)
    from_upper = neighbour(lower, -1)
    own = pl.pallas_call(owned_kernel, out_shape=shape((48, 4096), F32), compiler_params=params)(prod, links)
    result = pl.pallas_call(ghost_kernel, out_shape=shape((48, 4096), F32), compiler_params=params)(
        own, from_lower, from_upper, at
    )
    return result.reshape(3, 16, 4096)


def solution(mesh):
    in_specs = (
        P(None, AXES),
        P(AXES, None),
        P(None, AXES),
        P(None, AXES),
        P(None, None, AXES),
        P(None, AXES),
        P(None, None, AXES),
        P(None, AXES),
        P(AXES),
        P(AXES),
    )
    out_specs = P(None, None, AXES)
    return jax.shard_map(shards, mesh=mesh, in_specs=in_specs, out_specs=out_specs, check_vma=False)
```

```python
import jax
import jax.numpy as jnp
from jax import lax
from jax.experimental import pallas as pl
from jax.experimental.pallas import tpu as pltpu
from jax.sharding import PartitionSpec as P

F32 = jnp.float32
BF16 = jnp.bfloat16
I32 = jnp.int32
LANES = 128
WIDE = 256
AXES = ("row", "col")
NT = (((1,), (1,)), ((), ()))
VMEM_BYTES = 32 * 2**20


def split(x):
    high = x.astype(BF16)
    return high, (x - high.astype(F32)).astype(BF16)


def one_hot(low, iota):
    return jnp.where(iota == low.astype(F32).astype(BF16), jnp.ones((), BF16), jnp.zeros((), BF16))


def iota_of(columns):
    return lax.broadcasted_iota(I32, (WIDE, columns), 0).astype(F32).astype(BF16)


def choose(stacked, high, rows):
    high = jnp.broadcast_to(high, (8, high.shape[1]))
    out = [stacked[r : r + 8] for r in range(0, rows, 8)]
    for h in range(1, stacked.shape[0] // rows):
        here = high == h
        out = [jnp.where(here, stacked[rows * h + 8 * i : rows * h + 8 * i + 8], x) for i, x in enumerate(out)]
    return jnp.concatenate(out, 0)


def swap_blocks(x):
    row = lax.broadcasted_iota(I32, x.shape, 0) >> 2
    col = lax.broadcasted_iota(I32, x.shape, 1) >> 5
    out = x
    for d in range(1, 4):
        moved = pltpu.roll(pltpu.roll(x, 16 - 4 * d, 0), 32 * d, 1)
        out = jnp.where(((col - row) & 3) == d, moved, out)
    return out


def code(block):
    high = block.astype(BF16).astype(F32)
    rest = (block - high) / jnp.where(high != 0.0, high, 1.0)
    rest = jnp.clip(jnp.floor(rest * 2048.0 + 8.0), 0.0, 15.0)
    return high, rest[0:8] * 16.0 + rest[8:16]


def fill_pair(tab, h, first, second):
    base = 2 * tab.shape[0] // 3
    (high, rest), (high2, rest2) = code(first), code(second)
    tab[16 * h : 16 * h + 32, :] = jnp.concatenate([high, high2], 0).astype(BF16)
    tab[base + 8 * h : base + 8 * h + 16, :] = jnp.concatenate([rest, rest2], 0).astype(BF16)


def look_up(tab, hot, high):
    stacked = jnp.dot(tab[...], hot, preferred_element_type=F32)
    base = 2 * tab.shape[0] // 3
    value = choose(stacked[0:base], high, 16)
    both = choose(stacked[base:], high, 8)
    upper = jnp.floor(both * 0.0625)
    lower = both - 16.0 * upper
    unit, shift = 1.0 / 2048.0, 1.0 - 7.5 / 2048.0
    return jnp.concatenate([value[0:8] * (upper * unit + shift), value[8:16] * (lower * unit + shift)], 0)


def send_kernel(temp_hbm, index_hbm, out, tab, temp, index, sems):
    parts = 4
    width = temp.shape[1] // parts
    copies = [
        pltpu.make_async_copy(temp_hbm.at[:, pl.ds(i * width, width)], temp.at[:, pl.ds(i * width, width)], sems.at[i])
        for i in range(parts)
    ]
    copies.append(pltpu.make_async_copy(index_hbm, index, sems.at[parts]))
    for copy in copies:
        copy.start()
    iota = iota_of(WIDE)
    for h in range(temp.shape[1] // WIDE):
        if h * WIDE % width == 0:
            copies[h * WIDE // width].wait()
        if h % 2 == 0:
            fill_pair(tab, h, temp[:, h * WIDE : (h + 1) * WIDE], temp[:, (h + 1) * WIDE : (h + 2) * WIDE])
    copies[parts].wait()
    for j in range(index.shape[1] // WIDE):
        idx = index[0:1, j * WIDE : (j + 1) * WIDE]
        hot = one_hot(idx & (WIDE - 1), iota)
        got = look_up(tab, hot, idx >> 8)
        out[2 * j] = swap_blocks(got[:, 0:LANES])
        out[2 * j + 1] = swap_blocks(got[:, LANES:])


def main_kernel(
    arrived, slot_hbm, weight_hbm, disp_hbm, expansion_hbm, blocks, connect,
    prod, lower, upper,
    tab, tab3, slot, weight, disp, expansion, matrices, vec, sems,
):
    pairs = ((slot_hbm, slot), (weight_hbm, weight), (expansion_hbm, expansion), (disp_hbm, disp), (blocks, matrices))
    copies = [pltpu.make_async_copy(source, place, sems.at[i]) for i, (source, place) in enumerate(pairs)]
    for copy in copies:
        copy.start()
    extent = slot.shape[1]

    for h in range(0, arrived.shape[0] // 2, 2):
        tiles = [swap_blocks(arrived[2 * h + i]) for i in range(4)]
        fill_pair(tab, h, jnp.concatenate(tiles[0:2], 1), jnp.concatenate(tiles[2:4], 1))
    iota = iota_of(WIDE)
    for copy in copies[0:4]:
        copy.wait()

    for j in range(extent // WIDE):
        js = slice(j * WIDE, (j + 1) * WIDE)
        temp = jnp.zeros((16, WIDE), F32)
        for c in range(4):
            idx = slot[c : c + 1, js]
            hot = one_hot(idx & (WIDE - 1), iota)
            temp = temp + weight[c : c + 1, js] * look_up(tab, hot, idx >> 8)
        strain = temp / jnp.sqrt(1.0 + temp * temp)
        for a in range(3):
            d = disp[16 * a : 16 * a + 16, js].astype(F32)
            s = (d - expansion[a : a + 1, js] * strain).astype(BF16)
            tab3[j * 48 + a * 16 : j * 48 + a * 16 + 16, :] = s

    copies[4].wait()
    lane = lax.broadcasted_iota(I32, (16, LANES), 1) >> 5
    count = connect.shape[1] // WIDE

    def indices(p):
        return connect[0:1, p * WIDE : (p + 1) * WIDE]

    def gather(p):
        idx = indices(p)
        hot = one_hot(idx & (WIDE - 1), iota)
        return choose(jnp.dot(tab3[...], hot, preferred_element_type=F32), idx >> 8, 48)

    def multiply(p, got):
        pieces = []
        for half in range(2):
            x = [got[16 * a : 16 * a + 16, half * LANES : (half + 1) * LANES] for a in range(3)]
            y = []
            for u in range(4):
                v = [turn(x[a], a - u) for a in range(3)]
                v = jnp.where(lane == 0, v[0], jnp.where(lane == 1, v[1], v[2])).astype(BF16)
                one = jnp.dot(v[:, 0:96], matrices[p * 8 + half * 4 + u], preferred_element_type=F32)
                y.append(jnp.concatenate([one, jnp.zeros((16, 32), F32)], 1))
            rows = []
            for a in range(3):
                w = [turn(y[u], u - a) for u in range(4)]
                rows.append(jnp.where(lane == 0, w[0], jnp.where(lane == 1, w[1], jnp.where(lane == 2, w[2], w[3]))))
            pieces.append(jnp.concatenate(rows, 0))
        value = jnp.concatenate(pieces, 1)
        prod[:, p * WIDE : (p + 1) * WIDE] = value

    def ghosts(p, total):
        idx = indices(p)
        hot = one_hot(idx & (WIDE - 1), iota)
        value = prod[:, p * WIDE : (p + 1) * WIDE]
        high, low = split(jnp.where((idx >> 8) == extent // WIDE - 1, value, 0.0))
        return total + lax.dot_general(jnp.concatenate([high, low], 0), hot, NT, preferred_element_type=F32)

    total = jnp.zeros((96, WIDE), F32)
    for p in range(count):
        vec[:, p * WIDE : (p + 1) * WIDE] = gather(p)
    for p in range(count):
        multiply(p, vec[:, p * WIDE : (p + 1) * WIDE])
    for p in range(count):
        total = ghosts(p, total)
    total = total[0:48] + total[48:96]
    lower[...] = total[:, 0:LANES]
    upper[...] = total[:, LANES:]


def turn(x, blocks):
    return pltpu.roll(x, (32 * blocks) % LANES, 1) if blocks else x


def spread(x, idx, blocks):
    zero = jnp.zeros((), BF16)
    hot = one_hot(idx & (WIDE - 1), iota_of(WIDE))
    high = jnp.broadcast_to((idx >> 8).astype(F32).astype(BF16), x.shape)
    sides = [
        jnp.concatenate([jnp.where(high == jnp.array(h, BF16), part, zero) for h in range(blocks)], 0)
        for part in split(x)
    ]
    return lax.dot_general(
        jnp.concatenate(sides, 1), jnp.concatenate([hot, hot], 1), NT, preferred_element_type=F32
    )


def owned_kernel(prod, connect, out):
    blocks = out.shape[1] // WIDE
    total = None
    for p in range(connect.shape[1] // WIDE):
        ks = slice(p * WIDE, (p + 1) * WIDE)
        term = spread(prod[:, ks], connect[0:1, ks], blocks)
        total = term if total is None else total + term
    for h in range(blocks):
        out[:, h * WIDE : (h + 1) * WIDE] = total[48 * h : 48 * h + 48]


def ghost_kernel(own, from_lower, from_upper, at, out):
    blocks = out.shape[1] // WIDE
    total = spread(jnp.concatenate([from_lower[...], from_upper[...]], 1), at[...], blocks)
    for h in range(blocks):
        hs = slice(h * WIDE, (h + 1) * WIDE)
        out[:, hs] = own[:, hs] + total[48 * h : 48 * h + 48]


def neighbour(block, distance):
    count = lax.axis_size("col")
    return lax.ppermute(block, "col", [(i, (i + distance) % count) for i in range(count)])


def shards(temp_thermal, send_index, interp_slot, interp_weight, disp, expansion, tangent, connect, recv_lower, recv_upper):
    shape = jax.ShapeDtypeStruct
    here = pl.BlockSpec(memory_space=pltpu.VMEM)
    away = pl.BlockSpec(memory_space=pltpu.HBM)
    free = pl.BlockSpec(memory_space=pl.ANY)
    keep = lambda x: pltpu.with_memory_space_constraint(x, pltpu.HBM)
    params = pltpu.CompilerParams(vmem_limit_bytes=VMEM_BYTES)
    packed = pl.pallas_call(
        send_kernel,
        out_shape=shape((32, 16, LANES), F32),
        in_specs=[away, away],
        out_specs=here,
        scratch_shapes=[
            pltpu.VMEM((384, WIDE), BF16),
            pltpu.VMEM((16, 4096), F32),
            pltpu.VMEM((1, 4096), I32),
            pltpu.SemaphoreType.DMA((5,)),
        ],
        compiler_params=params,
    )(keep(temp_thermal), keep(send_index))
    arrived = lax.all_to_all(packed.reshape(128, 4, LANES), AXES, split_axis=0, concat_axis=0, tiled=True)
    arrived = arrived.reshape(32, 16, LANES)
    links = connect.T.reshape(1, 4096)
    blocks = jnp.transpose(tangent, (2, 1, 0))
    col = lax.axis_index("col")
    at = jnp.concatenate(
        [jnp.where(col > 0, recv_lower, -1), jnp.where(col < lax.axis_size("col") - 1, recv_upper, -1)]
    ).reshape(1, WIDE)
    prod, lower, upper = pl.pallas_call(
        main_kernel,
        out_shape=(shape((48, 4096), F32), shape((48, LANES), F32), shape((48, LANES), F32)),
        in_specs=[here, away, away, away, away, free, here],
        out_specs=(here, here, here),
        scratch_shapes=[
            pltpu.VMEM((384, WIDE), BF16),
            pltpu.VMEM((17 * 48, WIDE), BF16),
            pltpu.VMEM((4, 4352), I32),
            pltpu.VMEM((4, 4352), F32),
            pltpu.VMEM((48, 4352), BF16),
            pltpu.VMEM((3, 4352), F32),
            pltpu.VMEM((128, 96, 96), BF16),
            pltpu.VMEM((48, 4096), F32),
            pltpu.SemaphoreType.DMA((5,)),
        ],
        compiler_params=params,
    )(
        arrived, keep(interp_slot), keep(interp_weight), keep(disp.reshape(48, -1)), keep(expansion), blocks, links
    )
    from_lower = neighbour(upper, 1)
    from_upper = neighbour(lower, -1)
    own = pl.pallas_call(owned_kernel, out_shape=shape((48, 4096), F32), compiler_params=params)(prod, links)
    result = pl.pallas_call(ghost_kernel, out_shape=shape((48, 4096), F32), compiler_params=params)(
        own, from_lower, from_upper, at
    )
    return result.reshape(3, 16, 4096)


def solution(mesh):
    in_specs = (
        P(None, AXES),
        P(AXES, None),
        P(None, AXES),
        P(None, AXES),
        P(None, None, AXES),
        P(None, AXES),
        P(None, None, AXES),
        P(None, AXES),
        P(AXES),
        P(AXES),
    )
    out_specs = P(None, None, AXES)
    return jax.shard_map(shards, mesh=mesh, in_specs=in_specs, out_specs=out_specs, check_vma=False)
```

```python
import jax
import jax.numpy as jnp
from jax import lax
from jax.experimental import pallas as pl
from jax.experimental.pallas import tpu as pltpu
from jax.sharding import PartitionSpec as P

F32 = jnp.float32
BF16 = jnp.bfloat16
I32 = jnp.int32
LANES = 128
WIDE = 256
AXES = ("row", "col")
NT = (((1,), (1,)), ((), ()))
VMEM_BYTES = 32 * 2**20


def split(x):
    high = x.astype(BF16)
    return high, (x - high.astype(F32)).astype(BF16)


def one_hot(low, iota):
    return jnp.where(iota == low.astype(F32).astype(BF16), jnp.ones((), BF16), jnp.zeros((), BF16))


def iota_of(columns):
    return lax.broadcasted_iota(I32, (WIDE, columns), 0).astype(F32).astype(BF16)


def choose(stacked, high, rows):
    high = jnp.broadcast_to(high, (8, high.shape[1]))
    out = [stacked[r : r + 8] for r in range(0, rows, 8)]
    for h in range(1, stacked.shape[0] // rows):
        here = high == h
        out = [jnp.where(here, stacked[rows * h + 8 * i : rows * h + 8 * i + 8], x) for i, x in enumerate(out)]
    return jnp.concatenate(out, 0)


def swap_blocks(x):
    row = lax.broadcasted_iota(I32, x.shape, 0) >> 2
    col = lax.broadcasted_iota(I32, x.shape, 1) >> 5
    out = x
    for d in range(1, 4):
        moved = pltpu.roll(pltpu.roll(x, 16 - 4 * d, 0), 32 * d, 1)
        out = jnp.where(((col - row) & 3) == d, moved, out)
    return out


def code(block):
    high = block.astype(BF16).astype(F32)
    rest = (block - high) / jnp.where(high != 0.0, high, 1.0)
    rest = jnp.clip(jnp.floor(rest * 2048.0 + 8.0), 0.0, 15.0)
    return high, rest[0:8] * 16.0 + rest[8:16]


def fill_pair(tab, h, first, second):
    base = 2 * tab.shape[0] // 3
    (high, rest), (high2, rest2) = code(first), code(second)
    tab[16 * h : 16 * h + 32, :] = jnp.concatenate([high, high2], 0).astype(BF16)
    tab[base + 8 * h : base + 8 * h + 16, :] = jnp.concatenate([rest, rest2], 0).astype(BF16)


def look_up(tab, hot, high):
    stacked = jnp.dot(tab[...], hot, preferred_element_type=F32)
    base = 2 * tab.shape[0] // 3
    value = choose(stacked[0:base], high, 16)
    both = choose(stacked[base:], high, 8)
    upper = jnp.floor(both * 0.0625)
    lower = both - 16.0 * upper
    unit, shift = 1.0 / 2048.0, 1.0 - 7.5 / 2048.0
    return jnp.concatenate([value[0:8] * (upper * unit + shift), value[8:16] * (lower * unit + shift)], 0)


def send_kernel(temp_hbm, index_hbm, out, tab, temp, index, sems):
    parts = 4
    width = temp.shape[1] // parts
    copies = [
        pltpu.make_async_copy(temp_hbm.at[:, pl.ds(i * width, width)], temp.at[:, pl.ds(i * width, width)], sems.at[i])
        for i in range(parts)
    ]
    copies.append(pltpu.make_async_copy(index_hbm, index, sems.at[parts]))
    for copy in copies:
        copy.start()
    iota = iota_of(WIDE)
    for h in range(temp.shape[1] // WIDE):
        if h * WIDE % width == 0:
            copies[h * WIDE // width].wait()
        if h % 2 == 0:
            fill_pair(tab, h, temp[:, h * WIDE : (h + 1) * WIDE], temp[:, (h + 1) * WIDE : (h + 2) * WIDE])
    copies[parts].wait()
    for j in range(index.shape[1] // WIDE):
        idx = index[0:1, j * WIDE : (j + 1) * WIDE]
        hot = one_hot(idx & (WIDE - 1), iota)
        got = look_up(tab, hot, idx >> 8)
        out[2 * j] = swap_blocks(got[:, 0:LANES])
        out[2 * j + 1] = swap_blocks(got[:, LANES:])


def main_kernel(
    arrived, slot_hbm, weight_hbm, disp_hbm, expansion_hbm, blocks, connect,
    prod, near, far,
    tab, tab3, slot, weight, disp, expansion, matrices, vec, sems,
):
    pairs = ((slot_hbm, slot), (weight_hbm, weight), (expansion_hbm, expansion), (disp_hbm, disp), (blocks, matrices))
    copies = [pltpu.make_async_copy(source, place, sems.at[i]) for i, (source, place) in enumerate(pairs)]
    for copy in copies:
        copy.start()
    extent = slot.shape[1]

    for h in range(0, arrived.shape[0] // 2, 2):
        tiles = [swap_blocks(arrived[2 * h + i]) for i in range(4)]
        fill_pair(tab, h, jnp.concatenate(tiles[0:2], 1), jnp.concatenate(tiles[2:4], 1))
    iota = iota_of(WIDE)
    for copy in copies[0:4]:
        copy.wait()

    for j in range(extent // WIDE):
        js = slice(j * WIDE, (j + 1) * WIDE)
        temp = jnp.zeros((16, WIDE), F32)
        for c in range(4):
            idx = slot[c : c + 1, js]
            hot = one_hot(idx & (WIDE - 1), iota)
            temp = temp + weight[c : c + 1, js] * look_up(tab, hot, idx >> 8)
        strain = temp / jnp.sqrt(1.0 + temp * temp)
        for a in range(3):
            d = disp[16 * a : 16 * a + 16, js].astype(F32)
            s = (d - expansion[a : a + 1, js] * strain).astype(BF16)
            tab3[j * 48 + a * 16 : j * 48 + a * 16 + 16, :] = s

    copies[4].wait()
    lane = lax.broadcasted_iota(I32, (16, LANES), 1) >> 5
    count = connect.shape[1] // WIDE

    def indices(p):
        return connect[0:1, p * WIDE : (p + 1) * WIDE]

    def gather(p):
        idx = indices(p)
        hot = one_hot(idx & (WIDE - 1), iota)
        return choose(jnp.dot(tab3[...], hot, preferred_element_type=F32), idx >> 8, 48)

    def multiply(p, got):
        pieces = []
        for half in range(2):
            x = [got[16 * a : 16 * a + 16, half * LANES : (half + 1) * LANES] for a in range(3)]
            y = []
            for u in range(4):
                v = [turn(x[a], a - u) for a in range(3)]
                v = jnp.where(lane == 0, v[0], jnp.where(lane == 1, v[1], v[2])).astype(BF16)
                one = jnp.dot(v[:, 0:96], matrices[p * 8 + half * 4 + u], preferred_element_type=F32)
                y.append(jnp.concatenate([one, jnp.zeros((16, 32), F32)], 1))
            rows = []
            for a in range(3):
                w = [turn(y[u], u - a) for u in range(4)]
                rows.append(jnp.where(lane == 0, w[0], jnp.where(lane == 1, w[1], jnp.where(lane == 2, w[2], w[3]))))
            pieces.append(jnp.concatenate(rows, 0))
        value = jnp.concatenate(pieces, 1)
        prod[:, p * WIDE : (p + 1) * WIDE] = value

    def ghosts(p, total):
        idx = indices(p)
        hot = one_hot(idx & (WIDE - 1), iota)
        value = prod[:, p * WIDE : (p + 1) * WIDE]
        high, low = split(jnp.where((idx >> 8) == extent // WIDE - 1, value, 0.0))
        return total + lax.dot_general(jnp.concatenate([high, low], 0), hot, NT, preferred_element_type=F32)

    total = jnp.zeros((96, WIDE), F32)
    for p in range(count):
        vec[:, p * WIDE : (p + 1) * WIDE] = gather(p)
    for p in range(count):
        multiply(p, vec[:, p * WIDE : (p + 1) * WIDE])
    for p in range(count):
        total = ghosts(p, total)
    total = total[0:48] + total[48:96]
    even = lax.rem(lax.axis_index("col"), 2) == 0
    lower, upper = total[:, 0:LANES], total[:, LANES:]
    near[...] = jnp.where(even, upper, lower)
    far[...] = jnp.where(even, lower, upper)


def turn(x, blocks):
    return pltpu.roll(x, (32 * blocks) % LANES, 1) if blocks else x


def spread(x, idx, blocks):
    zero = jnp.zeros((), BF16)
    hot = one_hot(idx & (WIDE - 1), iota_of(WIDE))
    high = jnp.broadcast_to((idx >> 8).astype(F32).astype(BF16), x.shape)
    sides = [
        jnp.concatenate([jnp.where(high == jnp.array(h, BF16), part, zero) for h in range(blocks)], 0)
        for part in split(x)
    ]
    return lax.dot_general(
        jnp.concatenate(sides, 1), jnp.concatenate([hot, hot], 1), NT, preferred_element_type=F32
    )


def owned_kernel(prod, connect, out):
    blocks = out.shape[1] // WIDE
    total = None
    for p in range(connect.shape[1] // WIDE):
        ks = slice(p * WIDE, (p + 1) * WIDE)
        term = spread(prod[:, ks], connect[0:1, ks], blocks)
        total = term if total is None else total + term
    for h in range(blocks):
        out[:, h * WIDE : (h + 1) * WIDE] = total[48 * h : 48 * h + 48]


def ghost_kernel(own, near, far, at, out):
    blocks = out.shape[1] // WIDE
    total = spread(jnp.concatenate([near[...], far[...]], 1), at[...], blocks)
    for h in range(blocks):
        hs = slice(h * WIDE, (h + 1) * WIDE)
        out[:, hs] = own[:, hs] + total[48 * h : 48 * h + 48]


def swap(block, first):
    count = lax.axis_size("col")
    partner = list(range(count))
    for i in range(first, count - 1, 2):
        partner[i], partner[i + 1] = i + 1, i
    return lax.ppermute(block, "col", list(enumerate(partner)))


def shards(temp_thermal, send_index, interp_slot, interp_weight, disp, expansion, tangent, connect, recv_lower, recv_upper):
    shape = jax.ShapeDtypeStruct
    here = pl.BlockSpec(memory_space=pltpu.VMEM)
    away = pl.BlockSpec(memory_space=pltpu.HBM)
    free = pl.BlockSpec(memory_space=pl.ANY)
    keep = lambda x: pltpu.with_memory_space_constraint(x, pltpu.HBM)
    params = pltpu.CompilerParams(vmem_limit_bytes=VMEM_BYTES)
    packed = pl.pallas_call(
        send_kernel,
        out_shape=shape((32, 16, LANES), F32),
        in_specs=[away, away],
        out_specs=here,
        scratch_shapes=[
            pltpu.VMEM((384, WIDE), BF16),
            pltpu.VMEM((16, 4096), F32),
            pltpu.VMEM((1, 4096), I32),
            pltpu.SemaphoreType.DMA((5,)),
        ],
        compiler_params=params,
    )(keep(temp_thermal), keep(send_index))
    arrived = lax.all_to_all(packed.reshape(128, 4, LANES), AXES, split_axis=0, concat_axis=0, tiled=True)
    arrived = arrived.reshape(32, 16, LANES)
    links = connect.T.reshape(1, 4096)
    blocks = jnp.transpose(tangent, (2, 1, 0))
    col = lax.axis_index("col")
    even = col % 2 == 0
    edge = (col == 0) | (col == lax.axis_size("col") - 1)
    at = jnp.concatenate(
        [
            jnp.where(even, recv_upper, recv_lower),
            jnp.where(edge, -1, jnp.where(even, recv_lower, recv_upper)),
        ]
    ).reshape(1, WIDE)
    prod, near, far = pl.pallas_call(
        main_kernel,
        out_shape=(shape((48, 4096), F32), shape((48, LANES), F32), shape((48, LANES), F32)),
        in_specs=[here, away, away, away, away, free, here],
        out_specs=(here, here, here),
        scratch_shapes=[
            pltpu.VMEM((384, WIDE), BF16),
            pltpu.VMEM((17 * 48, WIDE), BF16),
            pltpu.VMEM((4, 4352), I32),
            pltpu.VMEM((4, 4352), F32),
            pltpu.VMEM((48, 4352), BF16),
            pltpu.VMEM((3, 4352), F32),
            pltpu.VMEM((128, 96, 96), BF16),
            pltpu.VMEM((48, 4096), F32),
            pltpu.SemaphoreType.DMA((5,)),
        ],
        compiler_params=params,
    )(
        arrived, keep(interp_slot), keep(interp_weight), keep(disp.reshape(48, -1)), keep(expansion), blocks, links
    )
    got_far = swap(far, 1)
    got_near = swap(near, 0)
    own = pl.pallas_call(owned_kernel, out_shape=shape((48, 4096), F32), compiler_params=params)(prod, links)
    result = pl.pallas_call(ghost_kernel, out_shape=shape((48, 4096), F32), compiler_params=params)(
        own, got_near, got_far, at
    )
    return result.reshape(3, 16, 4096)


def solution(mesh):
    in_specs = (
        P(None, AXES),
        P(AXES, None),
        P(None, AXES),
        P(None, AXES),
        P(None, None, AXES),
        P(None, AXES),
        P(None, None, AXES),
        P(None, AXES),
        P(AXES),
        P(AXES),
    )
    out_specs = P(None, None, AXES)
    return jax.shard_map(shards, mesh=mesh, in_specs=in_specs, out_specs=out_specs, check_vma=False)
```

```python
import jax
import jax.numpy as jnp
from jax import lax
from jax.experimental import pallas as pl
from jax.experimental.pallas import tpu as pltpu
from jax.sharding import PartitionSpec as P

F32 = jnp.float32
BF16 = jnp.bfloat16
I32 = jnp.int32
FINE = jnp.float8_e5m2
RAISE = 4096.0
LANES = 128
WIDE = 256
AXES = ("row", "col")
NT = (((1,), (1,)), ((), ()))
VMEM_BYTES = 32 * 2**20


def split(x):
    high = x.astype(BF16)
    return high, (x - high.astype(F32)).astype(BF16)


def one_hot(low, iota):
    return jnp.where(iota == low.astype(F32).astype(BF16), jnp.ones((), BF16), jnp.zeros((), BF16))


def iota_of(columns):
    return lax.broadcasted_iota(I32, (WIDE, columns), 0).astype(F32).astype(BF16)


def choose(stacked, high, rows):
    high = jnp.broadcast_to(high, (8, high.shape[1]))
    out = [stacked[r : r + 8] for r in range(0, rows, 8)]
    for h in range(1, stacked.shape[0] // rows):
        here = high == h
        out = [jnp.where(here, stacked[rows * h + 8 * i : rows * h + 8 * i + 8], x) for i, x in enumerate(out)]
    return jnp.concatenate(out, 0)


def swap_blocks(x):
    row = lax.broadcasted_iota(I32, x.shape, 0) >> 2
    col = lax.broadcasted_iota(I32, x.shape, 1) >> 5
    out = x
    for d in range(1, 4):
        moved = pltpu.roll(pltpu.roll(x, 16 - 4 * d, 0), 32 * d, 1)
        out = jnp.where(((col - row) & 3) == d, moved, out)
    return out


def code(block):
    high = block.astype(BF16).astype(F32)
    rest = (block - high) / jnp.where(high != 0.0, high, 1.0)
    rest = jnp.clip(jnp.floor(rest * 2048.0 + 8.0), 0.0, 15.0)
    return high, rest[0:8] * 16.0 + rest[8:16]


def fill_pair(tab, h, first, second):
    base = 2 * tab.shape[0] // 3
    (high, rest), (high2, rest2) = code(first), code(second)
    tab[16 * h : 16 * h + 32, :] = jnp.concatenate([high, high2], 0).astype(BF16)
    tab[base + 8 * h : base + 8 * h + 16, :] = jnp.concatenate([rest, rest2], 0).astype(BF16)


def look_up(tab, hot, high):
    stacked = jnp.dot(tab[...], hot, preferred_element_type=F32)
    base = 2 * tab.shape[0] // 3
    value = choose(stacked[0:base], high, 16)
    both = choose(stacked[base:], high, 8)
    upper = jnp.floor(both * 0.0625)
    lower = both - 16.0 * upper
    unit, shift = 1.0 / 2048.0, 1.0 - 7.5 / 2048.0
    return jnp.concatenate([value[0:8] * (upper * unit + shift), value[8:16] * (lower * unit + shift)], 0)


def send_kernel(temp_hbm, index_hbm, out, tab, temp, index, sems):
    parts = 4
    width = temp.shape[1] // parts
    copies = [
        pltpu.make_async_copy(temp_hbm.at[:, pl.ds(i * width, width)], temp.at[:, pl.ds(i * width, width)], sems.at[i])
        for i in range(parts)
    ]
    copies.append(pltpu.make_async_copy(index_hbm, index, sems.at[parts]))
    for copy in copies:
        copy.start()
    iota = iota_of(WIDE)
    for h in range(temp.shape[1] // WIDE):
        if h * WIDE % width == 0:
            copies[h * WIDE // width].wait()
        if h % 2 == 0:
            fill_pair(tab, h, temp[:, h * WIDE : (h + 1) * WIDE], temp[:, (h + 1) * WIDE : (h + 2) * WIDE])
    copies[parts].wait()
    for j in range(index.shape[1] // WIDE):
        idx = index[0:1, j * WIDE : (j + 1) * WIDE]
        hot = one_hot(idx & (WIDE - 1), iota)
        got = look_up(tab, hot, idx >> 8)
        out[2 * j] = swap_blocks(got[:, 0:LANES])
        out[2 * j + 1] = swap_blocks(got[:, LANES:])


def main_kernel(
    arrived, slot_hbm, weight_hbm, disp_hbm, expansion_hbm, blocks, connect,
    prod, near, far,
    tab, tab3, slot, weight, disp, expansion, matrices, vec, sems,
):
    pairs = ((slot_hbm, slot), (weight_hbm, weight), (expansion_hbm, expansion), (disp_hbm, disp), (blocks, matrices))
    copies = [pltpu.make_async_copy(source, place, sems.at[i]) for i, (source, place) in enumerate(pairs)]
    for copy in copies:
        copy.start()
    extent = slot.shape[1]

    for h in range(0, arrived.shape[0] // 2, 2):
        tiles = [swap_blocks(arrived[2 * h + i]) for i in range(4)]
        fill_pair(tab, h, jnp.concatenate(tiles[0:2], 1), jnp.concatenate(tiles[2:4], 1))
    iota = iota_of(WIDE)
    for copy in copies[0:4]:
        copy.wait()

    for j in range(extent // WIDE):
        js = slice(j * WIDE, (j + 1) * WIDE)
        temp = jnp.zeros((16, WIDE), F32)
        for c in range(4):
            idx = slot[c : c + 1, js]
            hot = one_hot(idx & (WIDE - 1), iota)
            temp = temp + weight[c : c + 1, js] * look_up(tab, hot, idx >> 8)
        strain = temp / jnp.sqrt(1.0 + temp * temp)
        for a in range(3):
            d = disp[16 * a : 16 * a + 16, js].astype(F32)
            s = (d - expansion[a : a + 1, js] * strain).astype(BF16)
            tab3[j * 48 + a * 16 : j * 48 + a * 16 + 16, :] = s

    copies[4].wait()
    lane = lax.broadcasted_iota(I32, (16, LANES), 1) >> 5
    count = connect.shape[1] // WIDE

    def indices(p):
        return connect[0:1, p * WIDE : (p + 1) * WIDE]

    def gather(p):
        idx = indices(p)
        hot = one_hot(idx & (WIDE - 1), iota)
        return choose(jnp.dot(tab3[...], hot, preferred_element_type=F32), idx >> 8, 48)

    def multiply(p, got):
        pieces = []
        for half in range(2):
            x = [got[16 * a : 16 * a + 16, half * LANES : (half + 1) * LANES] for a in range(3)]
            y = []
            for u in range(4):
                v = [turn(x[a], a - u) for a in range(3)]
                v = jnp.where(lane == 0, v[0], jnp.where(lane == 1, v[1], v[2])).astype(BF16)
                one = jnp.dot(v[:, 0:96], matrices[p * 8 + half * 4 + u], preferred_element_type=F32)
                y.append(jnp.concatenate([one, jnp.zeros((16, 32), F32)], 1))
            rows = []
            for a in range(3):
                w = [turn(y[u], u - a) for u in range(4)]
                rows.append(jnp.where(lane == 0, w[0], jnp.where(lane == 1, w[1], jnp.where(lane == 2, w[2], w[3]))))
            pieces.append(jnp.concatenate(rows, 0))
        value = jnp.concatenate(pieces, 1)
        prod[:, p * WIDE : (p + 1) * WIDE] = value

    def ghosts(p, total):
        idx = indices(p)
        hot = one_hot(idx & (WIDE - 1), iota)
        value = prod[:, p * WIDE : (p + 1) * WIDE]
        high, low = split(jnp.where((idx >> 8) == extent // WIDE - 1, value, 0.0))
        return total + lax.dot_general(jnp.concatenate([high, low], 0), hot, NT, preferred_element_type=F32)

    total = jnp.zeros((96, WIDE), F32)
    for p in range(count):
        vec[:, p * WIDE : (p + 1) * WIDE] = gather(p)
    for p in range(count):
        multiply(p, vec[:, p * WIDE : (p + 1) * WIDE])
    for p in range(count):
        total = ghosts(p, total)
    total = total[0:48] + total[48:96]
    even = lax.rem(lax.axis_index("col"), 2) == 0
    lower, upper = total[:, 0:LANES], total[:, LANES:]
    near[...] = jnp.where(even, upper, lower)
    far[...] = jnp.where(even, lower, upper)


def turn(x, blocks):
    return pltpu.roll(x, (32 * blocks) % LANES, 1) if blocks else x


def spread(x, idx, blocks):
    zero = jnp.zeros((), BF16)
    hot = one_hot(idx & (WIDE - 1), iota_of(WIDE))
    high = jnp.broadcast_to((idx >> 8).astype(F32).astype(BF16), x.shape)
    sides = [
        jnp.concatenate([jnp.where(high == jnp.array(h, BF16), part, zero) for h in range(blocks)], 0)
        for part in split(x)
    ]
    return lax.dot_general(
        jnp.concatenate(sides, 1), jnp.concatenate([hot, hot], 1), NT, preferred_element_type=F32
    )


def spread_parts(x, idx, blocks):
    zero = jnp.zeros((), BF16)
    hot = one_hot(idx & (WIDE - 1), iota_of(WIDE))
    high = jnp.broadcast_to((idx >> 8).astype(F32).astype(BF16), x.shape)
    first = x.astype(BF16)
    second = ((x - first.astype(F32)) * RAISE).astype(BF16)
    first, second = (
        jnp.concatenate([jnp.where(high == jnp.array(h, BF16), part, zero) for h in range(blocks)], 0)
        for part in (first, second)
    )
    return (
        lax.dot_general(first, hot, NT, preferred_element_type=F32),
        lax.dot_general(second.astype(FINE), hot.astype(FINE), NT, preferred_element_type=F32),
    )


def owned_kernel(prod, connect, out):
    blocks = out.shape[1] // WIDE
    first = second = None
    for p in range(connect.shape[1] // WIDE):
        ks = slice(p * WIDE, (p + 1) * WIDE)
        x, y = spread_parts(prod[:, ks], connect[0:1, ks], blocks)
        first = x if first is None else first + x
        second = y if second is None else second + y
    for h in range(blocks):
        rows = slice(48 * h, 48 * h + 48)
        out[:, h * WIDE : (h + 1) * WIDE] = first[rows] + second[rows] * (1.0 / RAISE)


def ghost_kernel(own, near, far, at, out):
    blocks = out.shape[1] // WIDE
    total = spread(jnp.concatenate([near[...], far[...]], 1), at[...], blocks)
    for h in range(blocks):
        hs = slice(h * WIDE, (h + 1) * WIDE)
        out[:, hs] = own[:, hs] + total[48 * h : 48 * h + 48]


def swap(block, first):
    count = lax.axis_size("col")
    partner = list(range(count))
    for i in range(first, count - 1, 2):
        partner[i], partner[i + 1] = i + 1, i
    return lax.ppermute(block, "col", list(enumerate(partner)))


def shards(temp_thermal, send_index, interp_slot, interp_weight, disp, expansion, tangent, connect, recv_lower, recv_upper):
    shape = jax.ShapeDtypeStruct
    here = pl.BlockSpec(memory_space=pltpu.VMEM)
    away = pl.BlockSpec(memory_space=pltpu.HBM)
    free = pl.BlockSpec(memory_space=pl.ANY)
    keep = lambda x: pltpu.with_memory_space_constraint(x, pltpu.HBM)
    params = pltpu.CompilerParams(vmem_limit_bytes=VMEM_BYTES)
    packed = pl.pallas_call(
        send_kernel,
        out_shape=shape((32, 16, LANES), F32),
        in_specs=[away, away],
        out_specs=here,
        scratch_shapes=[
            pltpu.VMEM((384, WIDE), BF16),
            pltpu.VMEM((16, 4096), F32),
            pltpu.VMEM((1, 4096), I32),
            pltpu.SemaphoreType.DMA((5,)),
        ],
        compiler_params=params,
    )(keep(temp_thermal), keep(send_index))
    arrived = lax.all_to_all(packed.reshape(128, 4, LANES), AXES, split_axis=0, concat_axis=0, tiled=True)
    arrived = arrived.reshape(32, 16, LANES)
    links = connect.T.reshape(1, 4096)
    blocks = jnp.transpose(tangent, (2, 1, 0))
    col = lax.axis_index("col")
    even = col % 2 == 0
    edge = (col == 0) | (col == lax.axis_size("col") - 1)
    at = jnp.concatenate(
        [
            jnp.where(even, recv_upper, recv_lower),
            jnp.where(edge, -1, jnp.where(even, recv_lower, recv_upper)),
        ]
    ).reshape(1, WIDE)
    prod, near, far = pl.pallas_call(
        main_kernel,
        out_shape=(shape((48, 4096), F32), shape((48, LANES), F32), shape((48, LANES), F32)),
        in_specs=[here, away, away, away, away, free, here],
        out_specs=(here, here, here),
        scratch_shapes=[
            pltpu.VMEM((384, WIDE), BF16),
            pltpu.VMEM((17 * 48, WIDE), BF16),
            pltpu.VMEM((4, 4352), I32),
            pltpu.VMEM((4, 4352), F32),
            pltpu.VMEM((48, 4352), BF16),
            pltpu.VMEM((3, 4352), F32),
            pltpu.VMEM((128, 96, 96), BF16),
            pltpu.VMEM((48, 4096), F32),
            pltpu.SemaphoreType.DMA((5,)),
        ],
        compiler_params=params,
    )(
        arrived, keep(interp_slot), keep(interp_weight), keep(disp.reshape(48, -1)), keep(expansion), blocks, links
    )
    got_far = swap(far, 1)
    got_near = swap(near, 0)
    own = pl.pallas_call(owned_kernel, out_shape=shape((48, 4096), F32), compiler_params=params)(prod, links)
    result = pl.pallas_call(ghost_kernel, out_shape=shape((48, 4096), F32), compiler_params=params)(
        own, got_near, got_far, at
    )
    return result.reshape(3, 16, 4096)


def solution(mesh):
    in_specs = (
        P(None, AXES),
        P(AXES, None),
        P(None, AXES),
        P(None, AXES),
        P(None, None, AXES),
        P(None, AXES),
        P(None, None, AXES),
        P(None, AXES),
        P(AXES),
        P(AXES),
    )
    out_specs = P(None, None, AXES)
    return jax.shard_map(shards, mesh=mesh, in_specs=in_specs, out_specs=out_specs, check_vma=False)
```

```python
import jax
import jax.numpy as jnp
from jax import lax
from jax.experimental import pallas as pl
from jax.experimental.pallas import tpu as pltpu
from jax.sharding import PartitionSpec as P

F32 = jnp.float32
BF16 = jnp.bfloat16
I32 = jnp.int32
SHORT = jnp.float8_e4m3fn
TOP = 384.0
FINE = jnp.float8_e5m2
RAISE = 4096.0
LANES = 128
WIDE = 256
AXES = ("row", "col")
NT = (((1,), (1,)), ((), ()))
VMEM_BYTES = 32 * 2**20


def split(x):
    high = x.astype(BF16)
    return high, (x - high.astype(F32)).astype(BF16)


def one_hot(low, iota):
    return jnp.where(iota == low.astype(F32).astype(BF16), jnp.ones((), BF16), jnp.zeros((), BF16))


def iota_of(columns):
    return lax.broadcasted_iota(I32, (WIDE, columns), 0).astype(F32).astype(BF16)


def choose(stacked, high, rows):
    high = jnp.broadcast_to(high, (8, high.shape[1]))
    out = [stacked[r : r + 8] for r in range(0, rows, 8)]
    for h in range(1, stacked.shape[0] // rows):
        here = high == h
        out = [jnp.where(here, stacked[rows * h + 8 * i : rows * h + 8 * i + 8], x) for i, x in enumerate(out)]
    return jnp.concatenate(out, 0)


def swap_blocks(x):
    row = lax.broadcasted_iota(I32, x.shape, 0) >> 2
    col = lax.broadcasted_iota(I32, x.shape, 1) >> 5
    out = x
    for d in range(1, 4):
        moved = pltpu.roll(pltpu.roll(x, 16 - 4 * d, 0), 32 * d, 1)
        out = jnp.where(((col - row) & 3) == d, moved, out)
    return out


def code(block):
    high = block.astype(BF16).astype(F32)
    rest = (block - high) / jnp.where(high != 0.0, high, 1.0)
    rest = jnp.clip(jnp.floor(rest * 2048.0 + 8.0), 0.0, 15.0)
    return high, rest[0:8] * 16.0 + rest[8:16]


def fill_pair(tab, h, first, second):
    base = 2 * tab.shape[0] // 3
    (high, rest), (high2, rest2) = code(first), code(second)
    tab[16 * h : 16 * h + 32, :] = jnp.concatenate([high, high2], 0).astype(BF16)
    tab[base + 8 * h : base + 8 * h + 16, :] = jnp.concatenate([rest, rest2], 0).astype(BF16)


def look_up(tab, hot, high):
    stacked = jnp.dot(tab[...], hot, preferred_element_type=F32)
    base = 2 * tab.shape[0] // 3
    value = choose(stacked[0:base], high, 16)
    both = choose(stacked[base:], high, 8)
    upper = jnp.floor(both * 0.0625)
    lower = both - 16.0 * upper
    unit, shift = 1.0 / 2048.0, 1.0 - 7.5 / 2048.0
    return jnp.concatenate([value[0:8] * (upper * unit + shift), value[8:16] * (lower * unit + shift)], 0)


def send_kernel(temp_hbm, index_hbm, out, tab, temp, index, sems):
    parts = 4
    width = temp.shape[1] // parts
    copies = [
        pltpu.make_async_copy(temp_hbm.at[:, pl.ds(i * width, width)], temp.at[:, pl.ds(i * width, width)], sems.at[i])
        for i in range(parts)
    ]
    copies.append(pltpu.make_async_copy(index_hbm, index, sems.at[parts]))
    for copy in copies:
        copy.start()
    iota = iota_of(WIDE)
    for h in range(temp.shape[1] // WIDE):
        if h * WIDE % width == 0:
            copies[h * WIDE // width].wait()
        if h % 2 == 0:
            fill_pair(tab, h, temp[:, h * WIDE : (h + 1) * WIDE], temp[:, (h + 1) * WIDE : (h + 2) * WIDE])
    copies[parts].wait()
    for j in range(index.shape[1] // WIDE):
        idx = index[0:1, j * WIDE : (j + 1) * WIDE]
        hot = one_hot(idx & (WIDE - 1), iota)
        got = look_up(tab, hot, idx >> 8)
        out[2 * j] = swap_blocks(got[:, 0:LANES])
        out[2 * j + 1] = swap_blocks(got[:, LANES:])


def main_kernel(
    arrived, slot_hbm, weight_hbm, disp_hbm, expansion_hbm, blocks, connect,
    prod, near, far,
    tab, tab3, slot, weight, disp, expansion, matrices, vec, sems,
):
    pairs = ((slot_hbm, slot), (weight_hbm, weight), (expansion_hbm, expansion), (disp_hbm, disp), (blocks, matrices))
    copies = [pltpu.make_async_copy(source, place, sems.at[i]) for i, (source, place) in enumerate(pairs)]
    for copy in copies:
        copy.start()
    extent = slot.shape[1]

    largest = jnp.max(jnp.abs(arrived[...]), axis=0)
    largest = jnp.max(jnp.max(largest, axis=1, keepdims=True), axis=0, keepdims=True)
    largest = jnp.where(largest > 0.0, largest, 1.0)
    back = largest * (1.0 / TOP)
    raise_by = TOP / largest
    for h in range(0, arrived.shape[0] // 2, 2):
        tiles = [swap_blocks(arrived[2 * h + i]) * raise_by for i in range(4)]
        block = jnp.concatenate([jnp.concatenate(tiles[0:2], 1), jnp.concatenate(tiles[2:4], 1)], 0)
        first = block.astype(SHORT)
        tab[16 * h : 16 * h + 32, 0:WIDE] = first
        tab[16 * h : 16 * h + 32, WIDE : 2 * WIDE] = (block - first.astype(F32)).astype(SHORT)
    iota = iota_of(WIDE)
    for copy in copies[0:4]:
        copy.wait()

    for j in range(extent // WIDE):
        js = slice(j * WIDE, (j + 1) * WIDE)
        temp = jnp.zeros((16, WIDE), F32)
        for c in range(4):
            idx = slot[c : c + 1, js]
            hot = one_hot(idx & (WIDE - 1), iota)
            hot = hot.astype(SHORT)
            stacked = jnp.dot(tab[...], jnp.concatenate([hot, hot], 0), preferred_element_type=F32)
            temp = temp + weight[c : c + 1, js] * choose(stacked, idx >> 8, 16)
        temp = temp * back
        strain = temp / jnp.sqrt(1.0 + temp * temp)
        for a in range(3):
            d = disp[16 * a : 16 * a + 16, js].astype(F32)
            s = (d - expansion[a : a + 1, js] * strain).astype(BF16)
            tab3[j * 48 + a * 16 : j * 48 + a * 16 + 16, :] = s

    copies[4].wait()
    lane = lax.broadcasted_iota(I32, (16, LANES), 1) >> 5
    count = connect.shape[1] // WIDE

    def indices(p):
        return connect[0:1, p * WIDE : (p + 1) * WIDE]

    def gather(p):
        idx = indices(p)
        hot = one_hot(idx & (WIDE - 1), iota)
        return choose(jnp.dot(tab3[...], hot, preferred_element_type=F32), idx >> 8, 48)

    def multiply(p, got):
        pieces = []
        for half in range(2):
            x = [got[16 * a : 16 * a + 16, half * LANES : (half + 1) * LANES] for a in range(3)]
            y = []
            for u in range(4):
                v = [turn(x[a], a - u) for a in range(3)]
                v = jnp.where(lane == 0, v[0], jnp.where(lane == 1, v[1], v[2])).astype(BF16)
                one = jnp.dot(v[:, 0:96], matrices[p * 8 + half * 4 + u], preferred_element_type=F32)
                y.append(jnp.concatenate([one, jnp.zeros((16, 32), F32)], 1))
            rows = []
            for a in range(3):
                w = [turn(y[u], u - a) for u in range(4)]
                rows.append(jnp.where(lane == 0, w[0], jnp.where(lane == 1, w[1], jnp.where(lane == 2, w[2], w[3]))))
            pieces.append(jnp.concatenate(rows, 0))
        value = jnp.concatenate(pieces, 1)
        prod[:, p * WIDE : (p + 1) * WIDE] = value

    def ghosts(p, total):
        idx = indices(p)
        hot = one_hot(idx & (WIDE - 1), iota)
        value = prod[:, p * WIDE : (p + 1) * WIDE]
        high, low = split(jnp.where((idx >> 8) == extent // WIDE - 1, value, 0.0))
        return total + lax.dot_general(jnp.concatenate([high, low], 0), hot, NT, preferred_element_type=F32)

    total = jnp.zeros((96, WIDE), F32)
    for p in range(count):
        vec[:, p * WIDE : (p + 1) * WIDE] = gather(p)
    for p in range(count):
        multiply(p, vec[:, p * WIDE : (p + 1) * WIDE])
    for p in range(count):
        total = ghosts(p, total)
    total = total[0:48] + total[48:96]
    even = lax.rem(lax.axis_index("col"), 2) == 0
    lower, upper = total[:, 0:LANES], total[:, LANES:]
    near[...] = jnp.where(even, upper, lower)
    far[...] = jnp.where(even, lower, upper)


def turn(x, blocks):
    return pltpu.roll(x, (32 * blocks) % LANES, 1) if blocks else x


def spread(x, idx, blocks):
    zero = jnp.zeros((), BF16)
    hot = one_hot(idx & (WIDE - 1), iota_of(WIDE))
    high = jnp.broadcast_to((idx >> 8).astype(F32).astype(BF16), x.shape)
    sides = [
        jnp.concatenate([jnp.where(high == jnp.array(h, BF16), part, zero) for h in range(blocks)], 0)
        for part in split(x)
    ]
    return lax.dot_general(
        jnp.concatenate(sides, 1), jnp.concatenate([hot, hot], 1), NT, preferred_element_type=F32
    )


def spread_parts(x, idx, blocks):
    zero = jnp.zeros((), BF16)
    hot = one_hot(idx & (WIDE - 1), iota_of(WIDE))
    high = jnp.broadcast_to((idx >> 8).astype(F32).astype(BF16), x.shape)
    first = x.astype(BF16)
    second = ((x - first.astype(F32)) * RAISE).astype(BF16)
    first, second = (
        jnp.concatenate([jnp.where(high == jnp.array(h, BF16), part, zero) for h in range(blocks)], 0)
        for part in (first, second)
    )
    return (
        lax.dot_general(first, hot, NT, preferred_element_type=F32),
        lax.dot_general(second.astype(FINE), hot.astype(FINE), NT, preferred_element_type=F32),
    )


def owned_kernel(prod, connect, out):
    blocks = out.shape[1] // WIDE
    first = second = None
    for p in range(connect.shape[1] // WIDE):
        ks = slice(p * WIDE, (p + 1) * WIDE)
        x, y = spread_parts(prod[:, ks], connect[0:1, ks], blocks)
        first = x if first is None else first + x
        second = y if second is None else second + y
    for h in range(blocks):
        rows = slice(48 * h, 48 * h + 48)
        out[:, h * WIDE : (h + 1) * WIDE] = first[rows] + second[rows] * (1.0 / RAISE)


def ghost_kernel(far, near, own, at, out):
    blocks = out.shape[1] // WIDE
    total = spread(jnp.concatenate([near[...], far[...]], 1), at[...], blocks)
    for h in range(blocks):
        hs = slice(h * WIDE, (h + 1) * WIDE)
        out[:, hs] = own[:, hs] + total[48 * h : 48 * h + 48]


def swap(block, first):
    count = lax.axis_size("col")
    partner = list(range(count))
    for i in range(first, count - 1, 2):
        partner[i], partner[i + 1] = i + 1, i
    return lax.ppermute(block, "col", list(enumerate(partner)))


def shards(temp_thermal, send_index, interp_slot, interp_weight, disp, expansion, tangent, connect, recv_lower, recv_upper):
    shape = jax.ShapeDtypeStruct
    here = pl.BlockSpec(memory_space=pltpu.VMEM)
    away = pl.BlockSpec(memory_space=pltpu.HBM)
    free = pl.BlockSpec(memory_space=pl.ANY)
    keep = lambda x: pltpu.with_memory_space_constraint(x, pltpu.HBM)
    params = pltpu.CompilerParams(vmem_limit_bytes=VMEM_BYTES)
    packed = pl.pallas_call(
        send_kernel,
        out_shape=shape((32, 16, LANES), F32),
        in_specs=[away, away],
        out_specs=here,
        scratch_shapes=[
            pltpu.VMEM((384, WIDE), BF16),
            pltpu.VMEM((16, 4096), F32),
            pltpu.VMEM((1, 4096), I32),
            pltpu.SemaphoreType.DMA((5,)),
        ],
        compiler_params=params,
    )(keep(temp_thermal), keep(send_index))
    arrived = lax.all_to_all(packed.reshape(128, 4, LANES), AXES, split_axis=0, concat_axis=0, tiled=True)
    arrived = arrived.reshape(32, 16, LANES)
    links = connect.T.reshape(1, 4096)
    blocks = jnp.transpose(tangent, (2, 1, 0))
    col = lax.axis_index("col")
    even = col % 2 == 0
    edge = (col == 0) | (col == lax.axis_size("col") - 1)
    at = jnp.concatenate(
        [
            jnp.where(even, recv_upper, recv_lower),
            jnp.where(edge, -1, jnp.where(even, recv_lower, recv_upper)),
        ]
    ).reshape(1, WIDE)
    prod, near, far = pl.pallas_call(
        main_kernel,
        out_shape=(shape((48, 4096), F32), shape((48, LANES), F32), shape((48, LANES), F32)),
        in_specs=[here, away, away, away, away, free, here],
        out_specs=(here, here, here),
        scratch_shapes=[
            pltpu.VMEM((256, 2 * WIDE), SHORT),
            pltpu.VMEM((17 * 48, WIDE), BF16),
            pltpu.VMEM((4, 4352), I32),
            pltpu.VMEM((4, 4352), F32),
            pltpu.VMEM((48, 4352), BF16),
            pltpu.VMEM((3, 4352), F32),
            pltpu.VMEM((128, 96, 96), BF16),
            pltpu.VMEM((48, 4096), F32),
            pltpu.SemaphoreType.DMA((5,)),
        ],
        compiler_params=params,
    )(
        arrived, keep(interp_slot), keep(interp_weight), keep(disp.reshape(48, -1)), keep(expansion), blocks, links
    )
    got_far = swap(far, 1)
    got_near = swap(near, 0)
    own = pl.pallas_call(owned_kernel, out_shape=shape((48, 4096), F32), compiler_params=params)(prod, links)
    result = pl.pallas_call(ghost_kernel, out_shape=shape((48, 4096), F32), compiler_params=params)(
        got_far, got_near, own, at
    )
    return result.reshape(3, 16, 4096)


def solution(mesh):
    in_specs = (
        P(None, AXES),
        P(AXES, None),
        P(None, AXES),
        P(None, AXES),
        P(None, None, AXES),
        P(None, AXES),
        P(None, None, AXES),
        P(None, AXES),
        P(AXES),
        P(AXES),
    )
    out_specs = P(None, None, AXES)
    return jax.shard_map(shards, mesh=mesh, in_specs=in_specs, out_specs=out_specs, check_vma=False)
```

```python
import jax
import jax.numpy as jnp
from jax import lax
from jax.experimental import pallas as pl
from jax.experimental.pallas import tpu as pltpu
from jax.sharding import PartitionSpec as P

F32 = jnp.float32
BF16 = jnp.bfloat16
I32 = jnp.int32
SHORT = jnp.float8_e4m3fn
TOP = 384.0
FINE = jnp.float8_e5m2
RAISE = 4096.0
LANES = 128
WIDE = 256
AXES = ("row", "col")
NT = (((1,), (1,)), ((), ()))
VMEM_BYTES = 32 * 2**20


def split(x):
    high = x.astype(BF16)
    return high, (x - high.astype(F32)).astype(BF16)


def one_hot(low, iota):
    return jnp.where(iota == low.astype(F32).astype(BF16), jnp.ones((), BF16), jnp.zeros((), BF16))


def iota_of(columns):
    return lax.broadcasted_iota(I32, (WIDE, columns), 0).astype(F32).astype(BF16)


def choose(stacked, high, rows):
    high = jnp.broadcast_to(high, (8, high.shape[1]))
    out = [stacked[r : r + 8] for r in range(0, rows, 8)]
    for h in range(1, stacked.shape[0] // rows):
        here = high == h
        out = [jnp.where(here, stacked[rows * h + 8 * i : rows * h + 8 * i + 8], x) for i, x in enumerate(out)]
    return jnp.concatenate(out, 0)


def swap_blocks(x):
    row = lax.broadcasted_iota(I32, x.shape, 0) >> 2
    col = lax.broadcasted_iota(I32, x.shape, 1) >> 5
    out = x
    for d in range(1, 4):
        moved = pltpu.roll(pltpu.roll(x, 16 - 4 * d, 0), 32 * d, 1)
        out = jnp.where(((col - row) & 3) == d, moved, out)
    return out


def code(block):
    high = block.astype(BF16).astype(F32)
    rest = (block - high) / jnp.where(high != 0.0, high, 1.0)
    rest = jnp.clip(jnp.floor(rest * 2048.0 + 8.0), 0.0, 15.0)
    return high, rest[0:8] * 16.0 + rest[8:16]


def fill_pair(tab, h, first, second):
    base = 2 * tab.shape[0] // 3
    (high, rest), (high2, rest2) = code(first), code(second)
    tab[16 * h : 16 * h + 32, :] = jnp.concatenate([high, high2], 0).astype(BF16)
    tab[base + 8 * h : base + 8 * h + 16, :] = jnp.concatenate([rest, rest2], 0).astype(BF16)


def look_up(tab, hot, high):
    stacked = jnp.dot(tab[...], hot, preferred_element_type=F32)
    base = 2 * tab.shape[0] // 3
    value = choose(stacked[0:base], high, 16)
    both = choose(stacked[base:], high, 8)
    upper = jnp.floor(both * 0.0625)
    lower = both - 16.0 * upper
    unit, shift = 1.0 / 2048.0, 1.0 - 7.5 / 2048.0
    return jnp.concatenate([value[0:8] * (upper * unit + shift), value[8:16] * (lower * unit + shift)], 0)


def send_kernel(temp_hbm, index_hbm, out, tab, temp, index, sems):
    parts = 4
    width = temp.shape[1] // parts
    copies = [
        pltpu.make_async_copy(temp_hbm.at[:, pl.ds(i * width, width)], temp.at[:, pl.ds(i * width, width)], sems.at[i])
        for i in range(parts)
    ]
    copies.append(pltpu.make_async_copy(index_hbm, index, sems.at[parts]))
    for copy in copies:
        copy.start()
    iota = iota_of(WIDE)
    for h in range(temp.shape[1] // WIDE):
        if h * WIDE % width == 0:
            copies[h * WIDE // width].wait()
        if h % 2 == 0:
            fill_pair(tab, h, temp[:, h * WIDE : (h + 1) * WIDE], temp[:, (h + 1) * WIDE : (h + 2) * WIDE])
    copies[parts].wait()
    for j in range(index.shape[1] // WIDE):
        idx = index[0:1, j * WIDE : (j + 1) * WIDE]
        hot = one_hot(idx & (WIDE - 1), iota)
        got = look_up(tab, hot, idx >> 8)
        out[2 * j] = swap_blocks(got[:, 0:LANES])
        out[2 * j + 1] = swap_blocks(got[:, LANES:])


def pick_kernel(disp_hbm, expansion_hbm, connect, picked, factor, disp, expansion, both, tab, sems):
    copies = [
        pltpu.make_async_copy(disp_hbm, disp, sems.at[0]),
        pltpu.make_async_copy(expansion_hbm, expansion, sems.at[1]),
    ]
    for copy in copies:
        copy.start()
    for copy in copies:
        copy.wait()
    blocks = disp.shape[1] // WIDE
    base = 48 * blocks
    high, low = split(expansion[...])
    both[...] = jnp.zeros(both.shape, F32)
    both[0:3, :] = high.astype(F32)
    both[3:6, :] = low.astype(F32)
    for h in range(blocks):
        tab[48 * h : 48 * h + 48, :] = disp[:, h * WIDE : (h + 1) * WIDE]
    for h in range(0, blocks, 2):
        first = both[:, h * WIDE : (h + 1) * WIDE]
        second = both[:, (h + 1) * WIDE : (h + 2) * WIDE] if h + 1 < blocks else jnp.zeros_like(first)
        tab[base + 8 * h : base + 8 * h + 16, :] = jnp.concatenate([first, second], 0).astype(BF16)
    iota = iota_of(WIDE)
    for p in range(connect.shape[1] // WIDE):
        ks = slice(p * WIDE, (p + 1) * WIDE)
        idx = connect[0:1, ks]
        stacked = jnp.dot(tab[...], one_hot(idx & (WIDE - 1), iota), preferred_element_type=F32)
        picked[:, ks] = choose(stacked[0:base], idx >> 8, 48).astype(BF16)
        parts = choose(stacked[base:], idx >> 8, 8)
        factor[:, ks] = parts + pltpu.roll(parts, 5, 0)


def raising(x):
    largest = jnp.max(jnp.max(jnp.abs(x), axis=1, keepdims=True), axis=0, keepdims=True)
    largest = jnp.where(largest > 0.0, largest, 1.0)
    return TOP / largest, largest * (1.0 / TOP)


def fill_short(tab, h, block):
    first = block.astype(SHORT)
    tab[16 * h : 16 * h + 32, 0:WIDE] = first
    tab[16 * h : 16 * h + 32, WIDE : 2 * WIDE] = (block - first.astype(F32)).astype(SHORT)


def main_kernel(
    arrived, slot_hbm, weight_hbm, picked_hbm, factor, blocks, connect,
    prod, near, far,
    tab, tab3, slot, weight, picked, matrices, heat, vec, sems,
):
    pairs = ((slot_hbm, slot), (weight_hbm, weight), (picked_hbm, picked), (blocks, matrices))
    copies = [pltpu.make_async_copy(source, place, sems.at[i]) for i, (source, place) in enumerate(pairs)]
    for copy in copies:
        copy.start()
    extent = slot.shape[1]

    up, down = raising(jnp.max(jnp.abs(arrived[...]), axis=0))
    for h in range(0, arrived.shape[0] // 2, 2):
        tiles = [swap_blocks(arrived[2 * h + i]) * up for i in range(4)]
        fill_short(tab, h, jnp.concatenate([jnp.concatenate(tiles[0:2], 1), jnp.concatenate(tiles[2:4], 1)], 0))
    iota = iota_of(WIDE)
    for copy in copies[0:2]:
        copy.wait()

    for j in range(extent // WIDE):
        js = slice(j * WIDE, (j + 1) * WIDE)
        temp = jnp.zeros((16, WIDE), F32)
        for c in range(4):
            idx = slot[c : c + 1, js]
            hot = one_hot(idx & (WIDE - 1), iota)
            hot = hot.astype(SHORT)
            stacked = jnp.dot(tab[...], jnp.concatenate([hot, hot], 0), preferred_element_type=F32)
            temp = temp + weight[c : c + 1, js] * choose(stacked, idx >> 8, 16)
        temp = temp * down
        heat[:, js] = temp / jnp.sqrt(1.0 + temp * temp)

    up, down = raising(heat[...])
    for h in range(0, extent // WIDE, 2):
        first = heat[:, h * WIDE : (h + 1) * WIDE] * up
        second = jnp.zeros_like(first)
        if h + 1 < extent // WIDE:
            second = heat[:, (h + 1) * WIDE : (h + 2) * WIDE] * up
        fill_short(tab3, h, jnp.concatenate([first, second], 0))

    copies[2].wait()
    copies[3].wait()
    lane = lax.broadcasted_iota(I32, (16, LANES), 1) >> 5
    count = connect.shape[1] // WIDE

    def indices(p):
        return connect[0:1, p * WIDE : (p + 1) * WIDE]

    def gather(p):
        idx = indices(p)
        hot = one_hot(idx & (WIDE - 1), iota).astype(SHORT)
        stacked = jnp.dot(tab3[...], jnp.concatenate([hot, hot], 0), preferred_element_type=F32)
        strain = choose(stacked, idx >> 8, 16) * down
        ks = slice(p * WIDE, (p + 1) * WIDE)
        shifted = [
            picked[16 * a : 16 * a + 16, ks].astype(F32) - factor[a : a + 1, ks] * strain for a in range(3)
        ]
        return jnp.concatenate(shifted, 0).astype(BF16).astype(F32)

    def multiply(p, got):
        pieces = []
        for half in range(2):
            x = [got[16 * a : 16 * a + 16, half * LANES : (half + 1) * LANES] for a in range(3)]
            y = []
            for u in range(4):
                v = [turn(x[a], a - u) for a in range(3)]
                v = jnp.where(lane == 0, v[0], jnp.where(lane == 1, v[1], v[2])).astype(BF16)
                one = jnp.dot(v[:, 0:96], matrices[p * 8 + half * 4 + u], preferred_element_type=F32)
                y.append(jnp.concatenate([one, jnp.zeros((16, 32), F32)], 1))
            rows = []
            for a in range(3):
                w = [turn(y[u], u - a) for u in range(4)]
                rows.append(jnp.where(lane == 0, w[0], jnp.where(lane == 1, w[1], jnp.where(lane == 2, w[2], w[3]))))
            pieces.append(jnp.concatenate(rows, 0))
        value = jnp.concatenate(pieces, 1)
        prod[:, p * WIDE : (p + 1) * WIDE] = value

    def ghosts(p, total):
        idx = indices(p)
        hot = one_hot(idx & (WIDE - 1), iota)
        value = prod[:, p * WIDE : (p + 1) * WIDE]
        high, low = split(jnp.where((idx >> 8) == extent // WIDE - 1, value, 0.0))
        return total + lax.dot_general(jnp.concatenate([high, low], 0), hot, NT, preferred_element_type=F32)

    total = jnp.zeros((96, WIDE), F32)
    for p in range(count):
        vec[:, p * WIDE : (p + 1) * WIDE] = gather(p)
    for p in range(count):
        multiply(p, vec[:, p * WIDE : (p + 1) * WIDE])
    for p in range(count):
        total = ghosts(p, total)
    total = total[0:48] + total[48:96]
    even = lax.rem(lax.axis_index("col"), 2) == 0
    lower, upper = total[:, 0:LANES], total[:, LANES:]
    near[...] = jnp.where(even, upper, lower)
    far[...] = jnp.where(even, lower, upper)


def turn(x, blocks):
    return pltpu.roll(x, (32 * blocks) % LANES, 1) if blocks else x


def spread(x, idx, blocks):
    zero = jnp.zeros((), BF16)
    hot = one_hot(idx & (WIDE - 1), iota_of(WIDE))
    high = jnp.broadcast_to((idx >> 8).astype(F32).astype(BF16), x.shape)
    sides = [
        jnp.concatenate([jnp.where(high == jnp.array(h, BF16), part, zero) for h in range(blocks)], 0)
        for part in split(x)
    ]
    return lax.dot_general(
        jnp.concatenate(sides, 1), jnp.concatenate([hot, hot], 1), NT, preferred_element_type=F32
    )


def spread_parts(x, idx, blocks):
    zero = jnp.zeros((), BF16)
    hot = one_hot(idx & (WIDE - 1), iota_of(WIDE))
    high = jnp.broadcast_to((idx >> 8).astype(F32).astype(BF16), x.shape)
    first = x.astype(BF16)
    second = ((x - first.astype(F32)) * RAISE).astype(BF16)
    first, second = (
        jnp.concatenate([jnp.where(high == jnp.array(h, BF16), part, zero) for h in range(blocks)], 0)
        for part in (first, second)
    )
    return (
        lax.dot_general(first, hot, NT, preferred_element_type=F32),
        lax.dot_general(second.astype(FINE), hot.astype(FINE), NT, preferred_element_type=F32),
    )


def owned_kernel(prod, connect, out):
    blocks = out.shape[1] // WIDE
    first = second = None
    for p in range(connect.shape[1] // WIDE):
        ks = slice(p * WIDE, (p + 1) * WIDE)
        x, y = spread_parts(prod[:, ks], connect[0:1, ks], blocks)
        first = x if first is None else first + x
        second = y if second is None else second + y
    for h in range(blocks):
        rows = slice(48 * h, 48 * h + 48)
        out[:, h * WIDE : (h + 1) * WIDE] = first[rows] + second[rows] * (1.0 / RAISE)


def ghost_kernel(far, near, own, at_lower, at_upper, out):
    col = lax.axis_index("col")
    even = lax.rem(col, 2) == 0
    edge = (col == 0) | (col == lax.axis_size("col") - 1)
    at_near = jnp.where(even, at_upper[...], at_lower[...])
    at_far = jnp.where(edge, -1, jnp.where(even, at_lower[...], at_upper[...]))
    blocks = out.shape[1] // WIDE
    total = spread(jnp.concatenate([near[...], far[...]], 1), jnp.concatenate([at_near, at_far], 1), blocks)
    for h in range(blocks):
        hs = slice(h * WIDE, (h + 1) * WIDE)
        out[:, hs] = own[:, hs] + total[48 * h : 48 * h + 48]


def swap(block, first):
    count = lax.axis_size("col")
    partner = list(range(count))
    for i in range(first, count - 1, 2):
        partner[i], partner[i + 1] = i + 1, i
    return lax.ppermute(block, "col", list(enumerate(partner)))


def shards(temp_thermal, send_index, interp_slot, interp_weight, disp, expansion, tangent, connect, recv_lower, recv_upper):
    shape = jax.ShapeDtypeStruct
    here = pl.BlockSpec(memory_space=pltpu.VMEM)
    away = pl.BlockSpec(memory_space=pltpu.HBM)
    free = pl.BlockSpec(memory_space=pl.ANY)
    keep = lambda x: pltpu.with_memory_space_constraint(x, pltpu.HBM)
    params = pltpu.CompilerParams(vmem_limit_bytes=VMEM_BYTES)
    packed = pl.pallas_call(
        send_kernel,
        out_shape=shape((32, 16, LANES), F32),
        in_specs=[away, away],
        out_specs=here,
        scratch_shapes=[
            pltpu.VMEM((384, WIDE), BF16),
            pltpu.VMEM((16, 4096), F32),
            pltpu.VMEM((1, 4096), I32),
            pltpu.SemaphoreType.DMA((5,)),
        ],
        compiler_params=params,
    )(keep(temp_thermal), keep(send_index))
    arrived = lax.all_to_all(packed.reshape(128, 4, LANES), AXES, split_axis=0, concat_axis=0, tiled=True)
    arrived = arrived.reshape(32, 16, LANES)
    links = connect.T.reshape(1, 4096)
    blocks = jnp.transpose(tangent, (2, 1, 0))
    picked, factor = pl.pallas_call(
        pick_kernel,
        out_shape=(pltpu.HBM((48, 4096), BF16), shape((8, 4096), F32)),
        in_specs=[away, away, here],
        out_specs=(here, here),
        scratch_shapes=[
            pltpu.VMEM((48, 4352), BF16),
            pltpu.VMEM((3, 4352), F32),
            pltpu.VMEM((8, 4352), F32),
            pltpu.VMEM((17 * 48 + 18 * 8, WIDE), BF16),
            pltpu.SemaphoreType.DMA((2,)),
        ],
        compiler_params=params,
    )(keep(disp.reshape(48, -1)), keep(expansion), links)
    prod, near, far = pl.pallas_call(
        main_kernel,
        out_shape=(shape((48, 4096), F32), shape((48, LANES), F32), shape((48, LANES), F32)),
        in_specs=[here, away, away, away, here, free, here],
        out_specs=(here, here, here),
        scratch_shapes=[
            pltpu.VMEM((256, 2 * WIDE), SHORT),
            pltpu.VMEM((18 * 16, 2 * WIDE), SHORT),
            pltpu.VMEM((4, 4352), I32),
            pltpu.VMEM((4, 4352), F32),
            pltpu.VMEM((48, 4096), BF16),
            pltpu.VMEM((128, 96, 96), BF16),
            pltpu.VMEM((16, 4352), F32),
            pltpu.VMEM((48, 4096), F32),
            pltpu.SemaphoreType.DMA((4,)),
        ],
        compiler_params=params,
    )(
        arrived, keep(interp_slot), keep(interp_weight), keep(picked), factor, blocks, links
    )
    got_far = swap(far, 1)
    got_near = swap(near, 0)
    own = pl.pallas_call(owned_kernel, out_shape=shape((48, 4096), F32), compiler_params=params)(prod, links)
    result = pl.pallas_call(ghost_kernel, out_shape=shape((48, 4096), F32), compiler_params=params)(
        got_far, got_near, own, recv_lower.reshape(1, LANES), recv_upper.reshape(1, LANES)
    )
    return result.reshape(3, 16, 4096)


def solution(mesh):
    in_specs = (
        P(None, AXES),
        P(AXES, None),
        P(None, AXES),
        P(None, AXES),
        P(None, None, AXES),
        P(None, AXES),
        P(None, None, AXES),
        P(None, AXES),
        P(AXES),
        P(AXES),
    )
    out_specs = P(None, None, AXES)
    return jax.shard_map(shards, mesh=mesh, in_specs=in_specs, out_specs=out_specs, check_vma=False)
```

```python
import jax
import jax.numpy as jnp
from jax import lax
from jax.experimental import pallas as pl
from jax.experimental.pallas import tpu as pltpu
from jax.sharding import PartitionSpec as P

F32 = jnp.float32
BF16 = jnp.bfloat16
I32 = jnp.int32
SHORT = jnp.float8_e4m3fn
TOP = 384.0
FINE = jnp.float8_e5m2
RAISE = 4096.0
LANES = 128
WIDE = 256
AXES = ("row", "col")
NT = (((1,), (1,)), ((), ()))
VMEM_BYTES = 32 * 2**20


def split(x):
    high = x.astype(BF16)
    return high, (x - high.astype(F32)).astype(BF16)


def one_hot(low, iota):
    return jnp.where(iota == low.astype(F32).astype(BF16), jnp.ones((), BF16), jnp.zeros((), BF16))


def iota_of(columns):
    return lax.broadcasted_iota(I32, (WIDE, columns), 0).astype(F32).astype(BF16)


def choose(stacked, high, rows):
    high = jnp.broadcast_to(high, (8, high.shape[1]))
    out = [stacked[r : r + 8] for r in range(0, rows, 8)]
    for h in range(1, stacked.shape[0] // rows):
        here = high == h
        out = [jnp.where(here, stacked[rows * h + 8 * i : rows * h + 8 * i + 8], x) for i, x in enumerate(out)]
    return jnp.concatenate(out, 0)


def swap_blocks(x):
    row = lax.broadcasted_iota(I32, x.shape, 0) >> 2
    col = lax.broadcasted_iota(I32, x.shape, 1) >> 5
    out = x
    for d in range(1, 4):
        moved = pltpu.roll(pltpu.roll(x, 16 - 4 * d, 0), 32 * d, 1)
        out = jnp.where(((col - row) & 3) == d, moved, out)
    return out


def code(block):
    high = block.astype(BF16).astype(F32)
    rest = (block - high) / jnp.where(high != 0.0, high, 1.0)
    rest = jnp.clip(jnp.floor(rest * 2048.0 + 8.0), 0.0, 15.0)
    return high, rest[0:8] * 16.0 + rest[8:16]


def fill_pair(tab, h, first, second):
    base = 2 * tab.shape[0] // 3
    (high, rest), (high2, rest2) = code(first), code(second)
    tab[16 * h : 16 * h + 32, :] = jnp.concatenate([high, high2], 0).astype(BF16)
    tab[base + 8 * h : base + 8 * h + 16, :] = jnp.concatenate([rest, rest2], 0).astype(BF16)


def look_up(tab, hot, high):
    stacked = jnp.dot(tab[...], hot, preferred_element_type=F32)
    base = 2 * tab.shape[0] // 3
    value = choose(stacked[0:base], high, 16)
    both = choose(stacked[base:], high, 8)
    upper = jnp.floor(both * 0.0625)
    lower = both - 16.0 * upper
    unit, shift = 1.0 / 2048.0, 1.0 - 7.5 / 2048.0
    return jnp.concatenate([value[0:8] * (upper * unit + shift), value[8:16] * (lower * unit + shift)], 0)


def send_kernel(temp_hbm, index_hbm, out, tab, temp, index, sems):
    parts = 4
    width = temp.shape[1] // parts
    copies = [
        pltpu.make_async_copy(temp_hbm.at[:, pl.ds(i * width, width)], temp.at[:, pl.ds(i * width, width)], sems.at[i])
        for i in range(parts)
    ]
    copies.append(pltpu.make_async_copy(index_hbm, index, sems.at[parts]))
    for copy in copies:
        copy.start()
    iota = iota_of(WIDE)
    for h in range(temp.shape[1] // WIDE):
        if h * WIDE % width == 0:
            copies[h * WIDE // width].wait()
        if h % 2 == 0:
            fill_pair(tab, h, temp[:, h * WIDE : (h + 1) * WIDE], temp[:, (h + 1) * WIDE : (h + 2) * WIDE])
    copies[parts].wait()
    for j in range(index.shape[1] // WIDE):
        idx = index[0:1, j * WIDE : (j + 1) * WIDE]
        hot = one_hot(idx & (WIDE - 1), iota)
        got = look_up(tab, hot, idx >> 8)
        out[2 * j] = swap_blocks(got[:, 0:LANES])
        out[2 * j + 1] = swap_blocks(got[:, LANES:])


def pick_kernel(disp_hbm, expansion_hbm, connect, picked_hbm, factor, disp, expansion, both, tab, picked, sems):
    copies = [
        pltpu.make_async_copy(disp_hbm, disp, sems.at[0]),
        pltpu.make_async_copy(expansion_hbm, expansion, sems.at[1]),
    ]
    for copy in copies:
        copy.start()
    for copy in copies:
        copy.wait()
    blocks = disp.shape[1] // WIDE
    base = 48 * blocks
    high, low = split(expansion[...])
    both[...] = jnp.zeros(both.shape, F32)
    both[0:3, :] = high.astype(F32)
    both[3:6, :] = low.astype(F32)
    for h in range(blocks):
        tab[48 * h : 48 * h + 48, :] = disp[:, h * WIDE : (h + 1) * WIDE]
    for h in range(0, blocks, 2):
        first = both[:, h * WIDE : (h + 1) * WIDE]
        second = both[:, (h + 1) * WIDE : (h + 2) * WIDE] if h + 1 < blocks else jnp.zeros_like(first)
        tab[base + 8 * h : base + 8 * h + 16, :] = jnp.concatenate([first, second], 0).astype(BF16)
    iota = iota_of(WIDE)
    for p in range(connect.shape[1] // WIDE):
        ks = slice(p * WIDE, (p + 1) * WIDE)
        idx = connect[0:1, ks]
        stacked = jnp.dot(tab[...], one_hot(idx & (WIDE - 1), iota), preferred_element_type=F32)
        picked[:, ks] = choose(stacked[0:base], idx >> 8, 48).astype(BF16)
        parts = choose(stacked[base:], idx >> 8, 8)
        factor[:, ks] = parts + pltpu.roll(parts, 5, 0)
        if p % 4 == 3:
            done = pl.ds((p - 3) * WIDE, 4 * WIDE)
            copies.append(pltpu.make_async_copy(picked.at[:, done], picked_hbm.at[:, done], sems.at[2 + p // 4]))
            copies[-1].start()
    for copy in copies[2:]:
        copy.wait()


def raising(x):
    largest = jnp.max(jnp.max(jnp.abs(x), axis=1, keepdims=True), axis=0, keepdims=True)
    largest = jnp.where(largest > 0.0, largest, 1.0)
    return TOP / largest, largest * (1.0 / TOP)


def fill_short(tab, h, block):
    first = block.astype(SHORT)
    tab[16 * h : 16 * h + 32, 0:WIDE] = first
    tab[16 * h : 16 * h + 32, WIDE : 2 * WIDE] = (block - first.astype(F32)).astype(SHORT)


def main_kernel(
    arrived, slot_hbm, weight_hbm, picked_hbm, factor, blocks, connect,
    prod, near, far,
    tab, tab3, slot, weight, picked, matrices, heat, vec, sems,
):
    pairs = ((slot_hbm, slot), (weight_hbm, weight), (picked_hbm, picked), (blocks, matrices))
    copies = [pltpu.make_async_copy(source, place, sems.at[i]) for i, (source, place) in enumerate(pairs)]
    for copy in copies:
        copy.start()
    extent = slot.shape[1]

    up, down = raising(jnp.max(jnp.abs(arrived[...]), axis=0))
    for h in range(0, arrived.shape[0] // 2, 2):
        tiles = [swap_blocks(arrived[2 * h + i]) * up for i in range(4)]
        fill_short(tab, h, jnp.concatenate([jnp.concatenate(tiles[0:2], 1), jnp.concatenate(tiles[2:4], 1)], 0))
    iota = iota_of(WIDE)
    for copy in copies[0:2]:
        copy.wait()

    for j in range(extent // WIDE):
        js = slice(j * WIDE, (j + 1) * WIDE)
        temp = jnp.zeros((16, WIDE), F32)
        for c in range(4):
            idx = slot[c : c + 1, js]
            hot = one_hot(idx & (WIDE - 1), iota)
            hot = hot.astype(SHORT)
            stacked = jnp.dot(tab[...], jnp.concatenate([hot, hot], 0), preferred_element_type=F32)
            temp = temp + weight[c : c + 1, js] * choose(stacked, idx >> 8, 16)
        temp = temp * down
        heat[:, js] = temp / jnp.sqrt(1.0 + temp * temp)

    up, down = raising(heat[...])
    for h in range(0, extent // WIDE, 2):
        first = heat[:, h * WIDE : (h + 1) * WIDE] * up
        second = jnp.zeros_like(first)
        if h + 1 < extent // WIDE:
            second = heat[:, (h + 1) * WIDE : (h + 2) * WIDE] * up
        fill_short(tab3, h, jnp.concatenate([first, second], 0))

    copies[2].wait()
    copies[3].wait()
    lane = lax.broadcasted_iota(I32, (16, LANES), 1) >> 5
    count = connect.shape[1] // WIDE

    def indices(p):
        return connect[0:1, p * WIDE : (p + 1) * WIDE]

    def gather(p):
        idx = indices(p)
        hot = one_hot(idx & (WIDE - 1), iota).astype(SHORT)
        stacked = jnp.dot(tab3[...], jnp.concatenate([hot, hot], 0), preferred_element_type=F32)
        strain = choose(stacked, idx >> 8, 16) * down
        ks = slice(p * WIDE, (p + 1) * WIDE)
        shifted = [
            picked[16 * a : 16 * a + 16, ks].astype(F32) - factor[a : a + 1, ks] * strain for a in range(3)
        ]
        return jnp.concatenate(shifted, 0).astype(BF16).astype(F32)

    def multiply(p, got):
        pieces = []
        for half in range(2):
            x = [got[16 * a : 16 * a + 16, half * LANES : (half + 1) * LANES] for a in range(3)]
            y = []
            for u in range(4):
                v = [turn(x[a], a - u) for a in range(3)]
                v = jnp.where(lane == 0, v[0], jnp.where(lane == 1, v[1], v[2])).astype(BF16)
                one = jnp.dot(v[:, 0:96], matrices[p * 8 + half * 4 + u], preferred_element_type=F32)
                y.append(jnp.concatenate([one, jnp.zeros((16, 32), F32)], 1))
            rows = []
            for a in range(3):
                w = [turn(y[u], u - a) for u in range(4)]
                rows.append(jnp.where(lane == 0, w[0], jnp.where(lane == 1, w[1], jnp.where(lane == 2, w[2], w[3]))))
            pieces.append(jnp.concatenate(rows, 0))
        value = jnp.concatenate(pieces, 1)
        prod[:, p * WIDE : (p + 1) * WIDE] = value

    def ghosts(p, total):
        idx = indices(p)
        hot = one_hot(idx & (WIDE - 1), iota)
        value = prod[:, p * WIDE : (p + 1) * WIDE]
        high, low = split(jnp.where((idx >> 8) == extent // WIDE - 1, value, 0.0))
        return total + lax.dot_general(jnp.concatenate([high, low], 0), hot, NT, preferred_element_type=F32)

    total = jnp.zeros((96, WIDE), F32)
    for p in range(count):
        vec[:, p * WIDE : (p + 1) * WIDE] = gather(p)
    for p in range(count):
        multiply(p, vec[:, p * WIDE : (p + 1) * WIDE])
    for p in range(count):
        total = ghosts(p, total)
    total = total[0:48] + total[48:96]
    even = lax.rem(lax.axis_index("col"), 2) == 0
    lower, upper = total[:, 0:LANES], total[:, LANES:]
    near[...] = jnp.where(even, upper, lower)
    far[...] = jnp.where(even, lower, upper)


def turn(x, blocks):
    return pltpu.roll(x, (32 * blocks) % LANES, 1) if blocks else x


def spread(x, idx, blocks):
    zero = jnp.zeros((), BF16)
    hot = one_hot(idx & (WIDE - 1), iota_of(WIDE))
    high = jnp.broadcast_to((idx >> 8).astype(F32).astype(BF16), x.shape)
    sides = [
        jnp.concatenate([jnp.where(high == jnp.array(h, BF16), part, zero) for h in range(blocks)], 0)
        for part in split(x)
    ]
    return lax.dot_general(
        jnp.concatenate(sides, 1), jnp.concatenate([hot, hot], 1), NT, preferred_element_type=F32
    )


def spread_parts(x, idx, blocks):
    zero = jnp.zeros((), BF16)
    hot = one_hot(idx & (WIDE - 1), iota_of(WIDE))
    high = jnp.broadcast_to((idx >> 8).astype(F32).astype(BF16), x.shape)
    first = x.astype(BF16)
    second = ((x - first.astype(F32)) * RAISE).astype(BF16)
    first, second = (
        jnp.concatenate([jnp.where(high == jnp.array(h, BF16), part, zero) for h in range(blocks)], 0)
        for part in (first, second)
    )
    return (
        lax.dot_general(first, hot, NT, preferred_element_type=F32),
        lax.dot_general(second.astype(FINE), hot.astype(FINE), NT, preferred_element_type=F32),
    )


def owned_kernel(prod, connect, out):
    blocks = out.shape[1] // WIDE
    first = second = None
    for p in range(connect.shape[1] // WIDE):
        ks = slice(p * WIDE, (p + 1) * WIDE)
        x, y = spread_parts(prod[:, ks], connect[0:1, ks], blocks)
        first = x if first is None else first + x
        second = y if second is None else second + y
    for h in range(blocks):
        rows = slice(48 * h, 48 * h + 48)
        out[:, h * WIDE : (h + 1) * WIDE] = first[rows] + second[rows] * (1.0 / RAISE)


def ghost_kernel(far, near, own, at_lower, at_upper, out):
    col = lax.axis_index("col")
    even = lax.rem(col, 2) == 0
    edge = (col == 0) | (col == lax.axis_size("col") - 1)
    at_near = jnp.where(even, at_upper[...], at_lower[...])
    at_far = jnp.where(edge, -1, jnp.where(even, at_lower[...], at_upper[...]))
    blocks = out.shape[1] // WIDE
    total = spread(jnp.concatenate([near[...], far[...]], 1), jnp.concatenate([at_near, at_far], 1), blocks)
    for h in range(blocks):
        hs = slice(h * WIDE, (h + 1) * WIDE)
        out[:, hs] = own[:, hs] + total[48 * h : 48 * h + 48]


def swap(block, first):
    count = lax.axis_size("col")
    partner = list(range(count))
    for i in range(first, count - 1, 2):
        partner[i], partner[i + 1] = i + 1, i
    return lax.ppermute(block, "col", list(enumerate(partner)))


def shards(temp_thermal, send_index, interp_slot, interp_weight, disp, expansion, tangent, connect, recv_lower, recv_upper):
    shape = jax.ShapeDtypeStruct
    here = pl.BlockSpec(memory_space=pltpu.VMEM)
    away = pl.BlockSpec(memory_space=pltpu.HBM)
    free = pl.BlockSpec(memory_space=pl.ANY)
    keep = lambda x: pltpu.with_memory_space_constraint(x, pltpu.HBM)
    params = pltpu.CompilerParams(vmem_limit_bytes=VMEM_BYTES)
    packed = pl.pallas_call(
        send_kernel,
        out_shape=shape((32, 16, LANES), F32),
        in_specs=[away, away],
        out_specs=here,
        scratch_shapes=[
            pltpu.VMEM((384, WIDE), BF16),
            pltpu.VMEM((16, 4096), F32),
            pltpu.VMEM((1, 4096), I32),
            pltpu.SemaphoreType.DMA((5,)),
        ],
        compiler_params=params,
    )(keep(temp_thermal), keep(send_index))
    arrived = lax.all_to_all(packed.reshape(128, 4, LANES), AXES, split_axis=0, concat_axis=0, tiled=True)
    arrived = arrived.reshape(32, 16, LANES)
    links = connect.T.reshape(1, 4096)
    blocks = jnp.transpose(tangent, (2, 1, 0))
    picked, factor = pl.pallas_call(
        pick_kernel,
        out_shape=(pltpu.HBM((48, 4096), BF16), shape((8, 4096), F32)),
        in_specs=[away, away, here],
        out_specs=(away, here),
        scratch_shapes=[
            pltpu.VMEM((48, 4352), BF16),
            pltpu.VMEM((3, 4352), F32),
            pltpu.VMEM((8, 4352), F32),
            pltpu.VMEM((17 * 48 + 18 * 8, WIDE), BF16),
            pltpu.VMEM((48, 4096), BF16),
            pltpu.SemaphoreType.DMA((6,)),
        ],
        compiler_params=params,
    )(keep(disp.reshape(48, -1)), keep(expansion), links)
    prod, near, far = pl.pallas_call(
        main_kernel,
        out_shape=(shape((48, 4096), F32), shape((48, LANES), F32), shape((48, LANES), F32)),
        in_specs=[here, away, away, away, here, free, here],
        out_specs=(here, here, here),
        scratch_shapes=[
            pltpu.VMEM((256, 2 * WIDE), SHORT),
            pltpu.VMEM((18 * 16, 2 * WIDE), SHORT),
            pltpu.VMEM((4, 4352), I32),
            pltpu.VMEM((4, 4352), F32),
            pltpu.VMEM((48, 4096), BF16),
            pltpu.VMEM((128, 96, 96), BF16),
            pltpu.VMEM((16, 4352), F32),
            pltpu.VMEM((48, 4096), F32),
            pltpu.SemaphoreType.DMA((4,)),
        ],
        compiler_params=params,
    )(
        arrived, keep(interp_slot), keep(interp_weight), keep(picked), factor, blocks, links
    )
    got_far = swap(far, 1)
    got_near = swap(near, 0)
    own = pl.pallas_call(owned_kernel, out_shape=shape((48, 4096), F32), compiler_params=params)(prod, links)
    result = pl.pallas_call(ghost_kernel, out_shape=shape((48, 4096), F32), compiler_params=params)(
        got_far, got_near, own, recv_lower.reshape(1, LANES), recv_upper.reshape(1, LANES)
    )
    return result.reshape(3, 16, 4096)


def solution(mesh):
    in_specs = (
        P(None, AXES),
        P(AXES, None),
        P(None, AXES),
        P(None, AXES),
        P(None, None, AXES),
        P(None, AXES),
        P(None, None, AXES),
        P(None, AXES),
        P(AXES),
        P(AXES),
    )
    out_specs = P(None, None, AXES)
    return jax.shard_map(shards, mesh=mesh, in_specs=in_specs, out_specs=out_specs, check_vma=False)
```
